512 devices in a mesh: filt: 16 (over x, z_hi, core), rows: 32 (over y, z_lo).
Axes of the slice: x: 4, y: 8, z: 8 (z_hi: 2, z_lo: 4; z = z_hi * 4 + z_lo), core: 2. Of those that a mesh axis runs over, the one named last changes fastest.
Arguments:
- images: bfloat16 [32, 1024, 512], P('rows', 'filt'), may hold values from -6 to 6
- filters: bfloat16 [1024, 9, 1024], P('filt'), may hold values from -0.0625 to 0.0625
- cotangent: bfloat16 [32, 1024, 512], P('rows', 'filt'), may hold values from -6 to 6
Outputs:
- output: bfloat16 [32, 1024, 512], P('rows', 'filt')
- input_grad: bfloat16 [32, 512, 1024], P('rows', 'filt')
- filter_grad: float32 [1024, 9, 1024], P('filt')
The draws below stay inside these ranges and needn't reach their ends.
All inputs are finite; a program needn't handle non-finite values.
Results may differ from the reference program's by a relative error of at most 0.001.
Values may be sent and summed in bfloat16 or wider, within the bound.
A program may use at most 64 MiB of HBM per device.

```python
import jax
import jax.numpy as jnp
from jax import lax

CIN = 1024
COUT = 1024
WIDTH = 512
HEIGHT = 32


def raised(array, key, source, target, shards_of, factor):
    def block_of(dim):
        return (jnp.arange(array.shape[dim]) // (array.shape[dim] // shards_of)).reshape((-1,) + (1,) * (array.ndim - 1 - dim))

    one_side = jax.random.permutation(key, shards_of)[block_of(target)]
    far = (block_of(target) + shards_of // 2) % shards_of
    return jnp.where((block_of(source) == one_side) | (block_of(source) == far), factor * array, array)


def block_scale(key, extent, split, low, largest):
    level = 1.0
    for axis_at, shards_of in split:
        heights = jax.random.uniform(jax.random.fold_in(jax.random.fold_in(key, 6), axis_at), (shards_of,), jnp.float32, low / len(split), largest / len(split))
        level = level * jnp.repeat(jnp.exp(heights), extent[axis_at] // shards_of).reshape((-1,) + (1,) * (len(extent) - 1 - axis_at))
    return level


def bell_draw(rng, dims, scale, bound, shards=(), held_as=jnp.bfloat16):
    array = scale * jax.random.normal(rng, dims, jnp.float32)
    if shards:
        array = array * block_scale(rng, dims, shards, -0.22, 0.18)
    return jnp.clip(array, -bound, bound).astype(held_as)


def gaussian_with(stream_key, extent, scale, limit, pieces, heavy, kind=jnp.bfloat16):
    array = scale * jax.random.normal(stream_key, extent, jnp.float32)
    if pieces:
        array = array * block_scale(stream_key, extent, pieces, -0.22, 0.18)
    return jnp.clip(raised(array, jax.random.fold_in(stream_key, 3), *heavy), -limit, limit).astype(kind)


def setup_inputs(seed: int = 0) -> dict:
    seeds = jax.random.split(jax.random.key(seed), 4)
    return {
        "images": bell_draw(seeds[0], (HEIGHT, CIN, WIDTH), 1.0, 6.0, ((0, 32), (1, 16))),
        "filters": bell_draw(seeds[1], (COUT, 9, CIN), (9 * CIN) ** -0.5, 0.0625, ((0, 16),)),
        "cotangent": gaussian_with(seeds[2], (HEIGHT, COUT, WIDTH), 1.0, 6.0, ((0, 32), (1, 16)), (1, 2, 16, 2.0)),
    }


def reference(images, filters, cotangent):
    height = images.shape[0]
    pad_spec = ((1, 1), (0, 0), (1, 1))
    image_full = jnp.pad(images.astype(jnp.float32), pad_spec)
    grad_full = jnp.pad(cotangent.astype(jnp.float32), pad_spec)
    weights = filters.astype(jnp.float32)
    highest = lax.Precision.HIGHEST

    def step_row(carry, index):
        image_rows = lax.dynamic_slice_in_dim(image_full, index, 3, 0)
        grad_rows = lax.dynamic_slice_in_dim(grad_full, index, 3, 0)
        centre = grad_rows[1, :, 1:1 + WIDTH]
        out_row = jnp.zeros((COUT, WIDTH), jnp.float32)
        back_row = jnp.zeros((WIDTH, CIN), jnp.float32)
        taps = []
        for a in range(3):
            for b in range(3):
                window = image_rows[a, :, b:b + WIDTH]
                tap_weight = weights[:, 3 * a + b, :]
                out_row = out_row + jnp.dot(tap_weight, window, precision=highest)
                grad_window = grad_rows[2 - a, :, 2 - b:2 - b + WIDTH]
                back_row = back_row + jnp.dot(grad_window.T, tap_weight, precision=highest)
                taps.append(jnp.dot(centre, window.T, precision=highest))
        carry = carry + jnp.stack(taps, axis=1)
        return (carry, (out_row.astype(jnp.bfloat16), back_row.astype(jnp.bfloat16)))
    start = jnp.zeros((COUT, 9, CIN), jnp.float32)
    total, (output, input_grad) = lax.scan(step_row, start, jnp.arange(height, dtype=jnp.int32))
    filter_grad = total / jnp.sqrt(jnp.float32(height * WIDTH))
    return (output, input_grad, filter_grad)
```

```python
import functools

import jax
import jax.numpy as jnp
from jax import lax
from jax.experimental import pallas as pl
from jax.experimental.pallas import tpu as pltpu
from jax.sharding import PartitionSpec as P

X, ZH, CORES = 4, 2, 2
Y, ZL = 8, 4
TAPS = 3
SCALE_ROWS = 16
TOP = 200.0
f32 = jnp.float32
bf16 = jnp.bfloat16


def shifted(value, by):
    if by == 0:
        return value
    width = value.shape[1]
    column = lax.broadcasted_iota(jnp.int32, value.shape, 1)
    rolled = pltpu.roll(value, by % width, 1)
    return jnp.where(column == (0 if by == 1 else width - 1), 0.0, rolled)


def scale_for(block):
    largest = jnp.max(jnp.abs(block), axis=(0, 1), keepdims=True)
    return (TOP / jnp.maximum(largest, 1e-30)).astype(bf16).astype(f32)


def encode(value, scale):
    t = value * scale
    t2 = t * t
    t4 = t2 * t2
    t8 = t4 * t4
    t16 = t8 * t8
    return jnp.where(t < 0.0, -t16, t16).astype(bf16)


def decode(code, inverse):
    c = code.astype(f32)
    a = jnp.abs(c)
    root = lax.rsqrt(lax.rsqrt(lax.rsqrt(lax.rsqrt(jnp.maximum(a, 1e-37)))))
    root = jnp.where(a < 1e-37, 0.0, root) * inverse
    return jnp.where(c < 0.0, -root, root)


def pack(value, scale):
    lanes = value.shape[1] // 2
    flat = jnp.concatenate([value[:, :lanes], value[:, lanes:]], axis=0)
    return encode(flat, scale), jnp.broadcast_to(scale, (SCALE_ROWS, lanes)).astype(bf16)


def unpack(code):
    rows = code.shape[0] - SCALE_ROWS
    inverse = 1.0 / code[rows : rows + 1, :].astype(f32)
    flat = decode(code[:rows, :], inverse)
    return jnp.concatenate([flat[: rows // 2], flat[rows // 2 :]], axis=1)


def kernel(
    img_ref, filt_ref, cot_ref, out_ref, ig_ref, fg_ref,
    F, F2, G, G2, cots, S, dF, codes, got, FIN, O, OR, IGB, IGR, IGX, IGS, IGZ,
    f_sem, a_send, a_recv, b_send, b_recv, p_send, p_recv, c_send, c_recv, h_send, h_recv,
    rs_send, rs_recv, o_send, o_recv, ig_send, ig_recv, fz_send, fz_recv, fy_send, fy_recv,
):
    f, r = lax.axis_index("filt"), lax.axis_index("rows")
    x, zh, core = f // (ZH * CORES), (f // CORES) % ZH, f % CORES
    y, q = r // ZL, r % ZL
    chans, width = img_ref.shape
    part = chans // ZL
    stack = TAPS * chans

    def dev(f_to, r_to):
        return {"filt": f_to, "rows": r_to}

    def x_peer(d):
        return dev(((x + d) % X) * (ZH * CORES) + zh * CORES + core, r)

    def zl_peer(d):
        return dev(f, y * ZL + (q + d) % ZL)

    def y_peer(d):
        return dev(f, ((y + d) % Y) * ZL + q)

    partner = f + CORES - 2 * CORES * zh
    sibling = f + 1 - 2 * core
    zh_dev, core_dev = dev(partner, r), dev(sibling, r)

    sends = []

    def send(src, dst, s_sem, r_sem, to):
        copy = pltpu.make_async_remote_copy(
            src_ref=src, dst_ref=dst, send_sem=s_sem, recv_sem=r_sem,
            device_id=to, device_id_type=pl.DeviceIdType.MESH,
        )
        copy.start()
        return copy

    def arrived(dst, r_sem):
        pltpu.make_async_remote_copy(
            src_ref=dst, dst_ref=dst, send_sem=r_sem, recv_sem=r_sem,
            device_id=core_dev, device_id_type=pl.DeviceIdType.MESH,
        ).wait_recv()

    load_f = pltpu.make_async_copy(filt_ref, F, f_sem)
    load_f.start()

    barrier = pltpu.get_barrier_semaphore()

    def greet(to):
        pl.semaphore_signal(barrier, inc=1, device_id=to, device_id_type=pl.DeviceIdType.MESH)

    fixed = [x_peer(d) for d in range(1, X)] + [zl_peer(d) for d in range(1, ZL)]
    fixed += [y_peer(d) for d in range(1, Y)] + [zh_dev, core_dev]
    for to in fixed:
        greet(to)

    @pl.when((y > 0) & (q == 0))
    def _():
        for k in range(1, ZL):
            greet(dev(f, (y - 1) * ZL + k))

    @pl.when((y > 0) & (q > 0) & (q < ZL - 1))
    def _():
        greet(dev(f, (y - 1) * ZL + ZL - 1))

    @pl.when((y < Y - 1) & (q == ZL - 1))
    def _():
        for k in range(ZL - 1):
            greet(dev(f, (y + 1) * ZL + k))

    @pl.when((y < Y - 1) & (q > 0) & (q < ZL - 1))
    def _():
        greet(dev(f, (y + 1) * ZL))

    def g_block(k):
        return G.at[pl.ds(pl.multiple_of(k * chans, chans), chans), :]

    def g2_rows(k, to=q):
        at = 8 * (k // 8) + (to + 4 * (k % 2) + (k % 8) // 2) % 8
        return pl.ds(pl.multiple_of(at * part, part), part)

    def g2_block(k):
        return G2.at[g2_rows(k), :]

    def g2_piece(k, row, to=q):
        return G2.at[g2_rows(k, to), pl.ds(pl.multiple_of(row * width, width), width)]

    g_block(f)[...] = img_ref[...]
    g2_piece(f, q)[...] = img_ref[pl.ds(pl.multiple_of(q * part, part), part), :]
    cots[q + 1] = cot_ref[...]

    below = jnp.where(q == 0, ZL - 1, jnp.where(q == ZL - 1, 0, 1))
    above = jnp.where(q == ZL - 1, ZL - 1, jnp.where(q == 0, 0, 1))
    others = jnp.where(y > 0, below, 0) + jnp.where(y < Y - 1, above, 0)
    pl.semaphore_wait(barrier, len(fixed) + others)

    for d in range(1, ZL):
        to = (q + d) % ZL
        sends.append(send(
            img_ref.at[pl.ds(pl.multiple_of(to * part, part), part), :], g2_piece(f, q, to),
            p_send.at[d], p_recv.at[d], zl_peer(d),
        ))

    def gather_first(block, s_sem, r_sem):
        mine = block(f)
        sends.append(send(mine, mine, s_sem.at[0], r_sem.at[0], zh_dev))
        for d in range(1, X):
            sends.append(send(mine, mine, s_sem.at[d], r_sem.at[d], x_peer(d)))
        sends.append(send(mine, mine, s_sem.at[4], r_sem.at[4], core_dev))

    def gather_second(block, s_sem, r_sem):
        other = block(partner)
        arrived(other, r_sem.at[0])
        for d in range(1, X):
            sends.append(send(other, other, s_sem.at[4 + d], r_sem.at[4 + d], x_peer(d)))
        sends.append(send(other, other, s_sem.at[8], r_sem.at[8], core_dev))

    def gather_third(block, s_sem, r_sem):
        for d in range(1, X):
            x_from = ((x - d) % X) * (ZH * CORES) + core
            for second in range(2):
                k = x_from + CORES * (zh if second == 0 else 1 - zh)
                theirs = block(k)
                arrived(theirs, r_sem.at[d + 4 * second])
                at = 9 + 2 * (d - 1) + second
                sends.append(send(theirs, theirs, s_sem.at[at], r_sem.at[at], core_dev))

    def gather_last(block, s_sem, r_sem):
        base = 1 - core
        arrived(block(sibling), r_sem.at[4])
        arrived(block(partner + 1 - 2 * core), r_sem.at[8])
        for d in range(1, X):
            x_from = ((x - d) % X) * (ZH * CORES) + base
            for second in range(2):
                k = x_from + CORES * (zh if second == 0 else 1 - zh)
                arrived(block(k), r_sem.at[9 + 2 * (d - 1) + second])

    for d in range(1, ZL):
        sends.append(send(cot_ref, cots.at[q + 1], c_send.at[d], c_recv.at[d], zl_peer(d)))

    up = (q == ZL - 1) & (y < Y - 1)
    down = (q == 0) & (y > 0)

    def halo_copies(side):
        edge, slot = (y + 1, 0) if side == 0 else (y - 1, ZL + 1)
        return [
            pltpu.make_async_remote_copy(
                src_ref=cot_ref, dst_ref=cots.at[slot], send_sem=h_send.at[side, k],
                recv_sem=h_recv.at[side], device_id=dev(f, edge * ZL + k),
                device_id_type=pl.DeviceIdType.MESH,
            )
            for k in range(ZL)
        ]

    @pl.when(up)
    def _():
        for copy in halo_copies(0):
            copy.start()

    @pl.when(down)
    def _():
        for copy in halo_copies(1):
            copy.start()

    gather_first(g_block, a_send, a_recv)

    for d in range(1, ZL):
        arrived(g2_piece(f, (q - d) % ZL), p_recv.at[d])
    gather_first(g2_block, b_send, b_recv)

    load_f.wait()
    for k in range(TAPS * TAPS):
        F2[chans * k : chans * (k + 1), :] = F[:, k, :]

    def build(j):
        value = cots[j].astype(f32)
        for b in range(TAPS):
            S[b * chans : (b + 1) * chans, j * width : (j + 1) * width] = shifted(value, b - 1).astype(bf16)

    for d in range(1, ZL):
        arrived(cots.at[(q - d) % ZL + 1], c_recv.at[d])

    @pl.when(y == 0)
    def _():
        cots[0] = jnp.zeros_like(cot_ref)

    @pl.when(y == Y - 1)
    def _():
        cots[ZL + 1] = jnp.zeros_like(cot_ref)

    @pl.when(y > 0)
    def _():
        arrived(cots.at[0], h_recv.at[0])

    @pl.when(y < Y - 1)
    def _():
        arrived(cots.at[ZL + 1], h_recv.at[1])

    for j in range(ZL + 2):
        build(j)

    gather_second(g2_block, b_send, b_recv)
    gather_second(g_block, a_send, a_recv)

    groups = X * ZH * CORES
    cols = width // groups
    half = width // 2
    for p in range(2):
        total = None
        for a in range(TAPS):
            at = pl.multiple_of((q + 2 - a) * width + p * half, half)
            term = lax.dot_general(
                S[:, pl.ds(at, half)], F2[a * stack : (a + 1) * stack, :],
                (((0,), (0,)), ((), ())), preferred_element_type=f32,
            )
            total = term if total is None else total + term
        for k in range(groups // 2):
            g = p * (groups // 2) + k
            IGB[g % CORES, g // (ZH * CORES), (g // CORES) % ZH] = total[cols * k : cols * (k + 1)]
    sends.append(send(IGB.at[1 - core], IGR, ig_send.at[0], ig_recv.at[0], core_dev))

    gather_third(g2_block, b_send, b_recv)
    gather_third(g_block, a_send, a_recv)

    gather_last(g2_block, b_send, b_recv)
    for a in range(TAPS):
        at = (2 - a) * width
        dF[a * stack : (a + 1) * stack, :] = lax.dot_general(
            S[:, at : at + ZL * width], G2[...], (((1,), (1,)), ((), ())), preferred_element_type=f32
        )
    rows = TAPS * stack // Y
    scale = scale_for(dF[...])
    for k in range(Y):
        code, tail = pack(dF[rows * k : rows * (k + 1), :], scale)
        codes[k, : 2 * rows, :] = code
        codes[k, 2 * rows :, :] = tail
    for d in range(1, Y):
        sends.append(send(codes.at[(y + d) % Y], got.at[d], rs_send.at[d], rs_recv.at[d], y_peer(d)))

    arrived(IGR, ig_recv.at[0])
    for k in range(X):
        IGB[core, k] = IGB[core, k] + IGR[k]
    for d in range(1, X):
        sends.append(send(IGB.at[core, (x + d) % X], IGX.at[d], ig_send.at[d], ig_recv.at[d], x_peer(d)))

    gather_last(g_block, a_send, a_recv)
    for a in (0, 2, 1):
        total = None
        taps = jnp.dot(F2[a * stack : (a + 1) * stack, :], G[...], preferred_element_type=f32)
        for b in range(TAPS):
            term = shifted(taps[b * chans : (b + 1) * chans], 1 - b)
            total = term if total is None else total + term
        O[a] = total

    def out_copy(a):
        return pltpu.make_async_remote_copy(
            src_ref=O.at[a], dst_ref=OR.at[a // 2], send_sem=o_send.at[a // 2], recv_sem=o_recv.at[a // 2],
            device_id=dev(f, r + 1 - a), device_id_type=pl.DeviceIdType.MESH,
        )

    @pl.when(r < Y * ZL - 1)
    def _():
        out_copy(0).start()

    @pl.when(r > 0)
    def _():
        out_copy(2).start()

    piece = dF[pl.ds(pl.multiple_of(y * rows, rows), rows), :]
    for d in range(1, Y):
        arrived(got.at[d], rs_recv.at[d])
        piece = piece + unpack(got[d])
    piece = piece / jnp.sqrt(f32(Y * ZL * width))
    code, tail = pack(piece, scale_for(piece))
    FIN[y, q, : 2 * rows, :] = code
    FIN[y, q, 2 * rows :, :] = tail
    for d in range(1, ZL):
        sends.append(send(FIN.at[y, q], FIN.at[y, q], fz_send.at[d], fz_recv.at[d], zl_peer(d)))

    IGS[...] = IGB[core, x]
    for d in range(1, X):
        arrived(IGX.at[d], ig_recv.at[d])
        IGS[...] = IGS[...] + IGX[d]
    sends.append(send(IGS.at[1 - zh], IGZ, ig_send.at[X], ig_recv.at[X], zh_dev))

    for d in range(1, ZL):
        arrived(FIN.at[y, (q - d) % ZL], fz_recv.at[d])

    lane_group = lax.broadcasted_iota(jnp.int32, (rows, 128), 1) // 16

    def result(at):
        quarters = [unpack(FIN[at, k]) for k in range(ZL)]
        for t in range(8):
            half_at, j = t // 4, t % 4
            mine = (lane_group + (8 - j)) % ZL
            tile = quarters[0][:, 128 * half_at : 128 * (half_at + 1)]
            for k in range(1, ZL):
                tile = jnp.where(mine == k, quarters[k][:, 128 * half_at : 128 * (half_at + 1)], tile)
            if j:
                tile = pltpu.roll(tile, 128 - 16 * j, 1)
            fg_ref[pl.ds(pl.multiple_of(at * rows, 8), rows), 128 * t : 128 * (t + 1)] = tile

    def ring(step, way):
        at = (y - (step - 1)) % Y if way == 0 else (y + (step - 1)) % Y
        if step < Y // 2:
            ref = FIN.at[at]
        else:
            ref = FIN.at[at, pl.ds(way * (ZL // 2), ZL // 2)]
        return send(ref, ref, fy_send.at[way, step], fy_recv.at[way, step], y_peer(1 if way == 0 else -1))

    def ring_arrived(step, way):
        at = (y - step) % Y if way == 0 else (y + step) % Y
        if step < Y // 2:
            ref = FIN.at[at]
        else:
            ref = FIN.at[at, pl.ds(way * (ZL // 2), ZL // 2)]
        arrived(ref, fy_recv.at[way, step])

    for step in range(1, Y // 2 + 1):
        for way in range(2):
            if step > 1:
                ring_arrived(step - 1, way)
            sends.append(ring(step, way))
        if step == 1:
            result(y)
            OUT = O.at[1]

            @pl.when(r > 0)
            def _():
                arrived(OR.at[0], o_recv.at[0])
                OUT[...] = OUT[...] + OR[0]

            @pl.when(r < Y * ZL - 1)
            def _():
                arrived(OR.at[1], o_recv.at[1])
                OUT[...] = OUT[...] + OR[1]

            out_ref[...] = OUT[...].astype(bf16)
            arrived(IGZ, ig_recv.at[X])
            ig_ref[...] = (IGS[zh] + IGZ[...]).astype(bf16)
        else:
            result((y - (step - 1)) % Y)
            result((y + (step - 1)) % Y)
    for way in range(2):
        ring_arrived(Y // 2, way)
    result((y + Y // 2) % Y)

    for copy in sends:
        copy.wait_send()

    @pl.when(up)
    def _():
        for copy in halo_copies(0):
            copy.wait_send()

    @pl.when(down)
    def _():
        for copy in halo_copies(1):
            copy.wait_send()

    @pl.when(r < Y * ZL - 1)
    def _():
        out_copy(0).wait_send()

    @pl.when(r > 0)
    def _():
        out_copy(2).wait_send()


def on_device(images, filters, cotangent):
    _, chans, width = images.shape
    taps, total = filters.shape[1:]
    groups = X * ZH * CORES
    cols = width // groups
    stack = taps * chans
    piece = stack // Y
    quarter = total // ZL
    dma = pltpu.SemaphoreType.DMA
    vmem = pltpu.VMEM
    any_spec = pl.BlockSpec(memory_space=pl.ANY)
    vmem_spec = pl.BlockSpec(memory_space=pltpu.VMEM)
    code = (2 * piece + SCALE_ROWS, quarter // 2)
    output, input_grad, grad = pl.pallas_call(
        kernel,
        out_shape=(
            jax.ShapeDtypeStruct((chans, width), bf16),
            jax.ShapeDtypeStruct((cols, total), bf16),
            jax.ShapeDtypeStruct((stack, total), f32),
        ),
        in_specs=[vmem_spec, any_spec, vmem_spec],
        out_specs=(vmem_spec, vmem_spec, vmem_spec),
        scratch_shapes=[
            vmem((chans, taps, total), bf16),
            vmem((stack, total), bf16),
            vmem((total, width), bf16),
            vmem((quarter, ZL * width), bf16),
            vmem((ZL + 2, chans, width), bf16),
            vmem((TAPS * chans, (ZL + 2) * width), bf16),
            vmem((stack, quarter), f32),
            vmem((Y,) + code, bf16),
            vmem((Y,) + code, bf16),
            vmem((Y, ZL) + code, bf16),
            vmem((TAPS, chans, width), f32),
            vmem((2, chans, width), f32),
            vmem((CORES, X, ZH, cols, total), f32),
            vmem((X, ZH, cols, total), f32),
            vmem((X, ZH, cols, total), f32),
            vmem((ZH, cols, total), f32),
            vmem((cols, total), f32),
            dma,
            dma((15,)), dma((15,)),
            dma((15,)), dma((15,)),
            dma((ZL,)), dma((ZL,)),
            dma((ZL,)), dma((ZL,)),
            dma((2, ZL)), dma((2,)),
            dma((Y,)), dma((Y,)),
            dma((2,)), dma((2,)),
            dma((X + 1,)), dma((X + 1,)),
            dma((ZL,)), dma((ZL,)),
            dma((2, Y)), dma((2, Y)),
        ],
        compiler_params=pltpu.CompilerParams(
            collective_id=0, has_side_effects=True, vmem_limit_bytes=48 * 1024 * 1024
        ),
    )(images[0], filters, cotangent[0])
    grad = jnp.transpose(grad.reshape(taps, chans, total), (1, 0, 2))
    return output[None], input_grad[None], grad


def solution(mesh):
    return jax.shard_map(
        on_device,
        mesh=mesh,
        in_specs=(P("rows", "filt", None), P("filt", None, None), P("rows", "filt", None)),
        out_specs=(P("rows", "filt", None), P("rows", "filt", None), P("filt", None, None)),
        check_vma=False,
    )
```

```python
import functools

import jax
import jax.numpy as jnp
from jax import lax
from jax.experimental import pallas as pl
from jax.experimental.pallas import tpu as pltpu
from jax.sharding import PartitionSpec as P

X, ZH, CORES = 4, 2, 2
Y, ZL = 8, 4
TAPS = 3
SCALE_ROWS = 16
TOP = 200.0
f32 = jnp.float32
bf16 = jnp.bfloat16


def shifted(value, by):
    if by == 0:
        return value
    width = value.shape[1]
    column = lax.broadcasted_iota(jnp.int32, value.shape, 1)
    rolled = pltpu.roll(value, by % width, 1)
    return jnp.where(column == (0 if by == 1 else width - 1), 0.0, rolled)


def scale_for(block):
    largest = jnp.max(jnp.abs(block), axis=(0, 1), keepdims=True)
    return (TOP / jnp.maximum(largest, 1e-30)).astype(bf16).astype(f32)


def encode(value, scale):
    t = value * scale
    t2 = t * t
    t4 = t2 * t2
    t8 = t4 * t4
    t16 = t8 * t8
    return jnp.where(t < 0.0, -t16, t16).astype(bf16)


def decode(code, inverse):
    c = code.astype(f32)
    a = jnp.abs(c)
    root = lax.rsqrt(lax.rsqrt(lax.rsqrt(lax.rsqrt(jnp.maximum(a, 1e-37)))))
    root = jnp.where(a < 1e-37, 0.0, root) * inverse
    return jnp.where(c < 0.0, -root, root)


def pack(value, scale):
    lanes = value.shape[1] // 2
    flat = jnp.concatenate([value[:, :lanes], value[:, lanes:]], axis=0)
    return encode(flat, scale), jnp.broadcast_to(scale, (SCALE_ROWS, lanes)).astype(bf16)


def unpack(code):
    rows = code.shape[0] - SCALE_ROWS
    inverse = 1.0 / code[rows : rows + 1, :].astype(f32)
    flat = decode(code[:rows, :], inverse)
    return jnp.concatenate([flat[: rows // 2], flat[rows // 2 :]], axis=1)


def kernel(
    img_ref, filt_ref, cot_ref, out_ref, ig_ref, fg_ref,
    F2, G, G2, cots, S, dF, codes, got, FIN, O, OR, IGB, IGR, IGX, IGS, IGZ,
    f_sem, a_send, a_recv, b_send, b_recv, p_send, p_recv, c_send, c_recv, h_send, h_recv,
    rs_send, rs_recv, o_send, o_recv, ig_send, ig_recv, fz_send, fz_recv, fy_send, fy_recv,
):
    f, r = lax.axis_index("filt"), lax.axis_index("rows")
    x, zh, core = f // (ZH * CORES), (f // CORES) % ZH, f % CORES
    y, q = r // ZL, r % ZL
    chans, width = img_ref.shape
    part = chans // ZL
    stack = TAPS * chans

    def dev(f_to, r_to):
        return {"filt": f_to, "rows": r_to}

    def x_peer(d):
        return dev(((x + d) % X) * (ZH * CORES) + zh * CORES + core, r)

    def zl_peer(d):
        return dev(f, y * ZL + (q + d) % ZL)

    def y_peer(d):
        return dev(f, ((y + d) % Y) * ZL + q)

    partner = f + CORES - 2 * CORES * zh
    sibling = f + 1 - 2 * core
    zh_dev, core_dev = dev(partner, r), dev(sibling, r)

    sends = []

    def zh_peer(d):
        return dev(partner, y * ZL + (q + d) % ZL)

    def send(src, dst, s_sem, r_sem, to):
        copy = pltpu.make_async_remote_copy(
            src_ref=src, dst_ref=dst, send_sem=s_sem, recv_sem=r_sem,
            device_id=to, device_id_type=pl.DeviceIdType.MESH,
        )
        copy.start()
        return copy

    def arrived(dst, r_sem):
        pltpu.make_async_remote_copy(
            src_ref=dst, dst_ref=dst, send_sem=r_sem, recv_sem=r_sem,
            device_id=core_dev, device_id_type=pl.DeviceIdType.MESH,
        ).wait_recv()

    load_f = pltpu.make_async_copy(filt_ref, F2, f_sem)
    load_f.start()

    barrier = pltpu.get_barrier_semaphore()

    def greet(to):
        pl.semaphore_signal(barrier, inc=1, device_id=to, device_id_type=pl.DeviceIdType.MESH)

    fixed = [x_peer(d) for d in range(1, X)] + [zl_peer(d) for d in range(1, ZL)]
    fixed += [y_peer(d) for d in range(1, Y)] + [core_dev] + [zh_peer(d) for d in range(ZL)]
    for to in fixed:
        greet(to)

    @pl.when((y > 0) & (q == 0))
    def _():
        for k in range(1, ZL):
            greet(dev(f, (y - 1) * ZL + k))

    @pl.when((y > 0) & (q > 0) & (q < ZL - 1))
    def _():
        greet(dev(f, (y - 1) * ZL + ZL - 1))

    @pl.when((y < Y - 1) & (q == ZL - 1))
    def _():
        for k in range(ZL - 1):
            greet(dev(f, (y + 1) * ZL + k))

    @pl.when((y < Y - 1) & (q > 0) & (q < ZL - 1))
    def _():
        greet(dev(f, (y + 1) * ZL))

    def g_block(k):
        return G.at[pl.ds(pl.multiple_of(k * chans, chans), chans), :]

    def g2_rows(k, to=q):
        at = 8 * (k // 8) + (to + 4 * (k % 2) + (k % 8) // 2) % 8
        return pl.ds(pl.multiple_of(at * part, part), part)

    def g2_block(k):
        return G2.at[g2_rows(k), :]

    def g2_piece(k, row, to=q):
        return G2.at[g2_rows(k, to), pl.ds(pl.multiple_of(row * width, width), width)]

    g_block(f)[...] = img_ref[...]
    g2_piece(f, q)[...] = img_ref[pl.ds(pl.multiple_of(q * part, part), part), :]
    cots[q + 1] = cot_ref[...]

    below = jnp.where(q == 0, ZL - 1, jnp.where(q == ZL - 1, 0, 1))
    above = jnp.where(q == ZL - 1, ZL - 1, jnp.where(q == 0, 0, 1))
    others = jnp.where(y > 0, below, 0) + jnp.where(y < Y - 1, above, 0)
    pl.semaphore_wait(barrier, len(fixed) + others)

    for d in list(range(ZL, 2 * ZL)) + list(range(1, ZL)):
        to = (q + d) % ZL
        sends.append(send(
            img_ref.at[pl.ds(pl.multiple_of(to * part, part), part), :], g2_piece(f, q, to),
            p_send.at[d], p_recv.at[d], zl_peer(d) if d < ZL else zh_peer(d),
        ))

    def gather_own(block, s_sem, r_sem):
        mine = block(f)
        for d in range(1, X):
            sends.append(send(mine, mine, s_sem.at[d], r_sem.at[d], x_peer(d)))
        sends.append(send(mine, mine, s_sem.at[4], r_sem.at[4], core_dev))

    def gather_other(block, s_sem, r_sem):
        other = block(partner)
        for d in range(1, X):
            sends.append(send(other, other, s_sem.at[4 + d], r_sem.at[4 + d], x_peer(d)))
        sends.append(send(other, other, s_sem.at[8], r_sem.at[8], core_dev))

    def gather_third(block, s_sem, r_sem):
        for d in range(1, X):
            x_from = ((x - d) % X) * (ZH * CORES) + core
            for second in range(2):
                k = x_from + CORES * (zh if second == 0 else 1 - zh)
                theirs = block(k)
                arrived(theirs, r_sem.at[d + 4 * second])
                at = 9 + 2 * (d - 1) + second
                sends.append(send(theirs, theirs, s_sem.at[at], r_sem.at[at], core_dev))

    def gather_last(block, s_sem, r_sem):
        base = 1 - core
        arrived(block(sibling), r_sem.at[4])
        arrived(block(partner + 1 - 2 * core), r_sem.at[8])
        for d in range(1, X):
            x_from = ((x - d) % X) * (ZH * CORES) + base
            for second in range(2):
                k = x_from + CORES * (zh if second == 0 else 1 - zh)
                arrived(block(k), r_sem.at[9 + 2 * (d - 1) + second])

    for d in range(1, ZL):
        sends.append(send(cot_ref, cots.at[q + 1], c_send.at[d], c_recv.at[d], zl_peer(d)))

    up = (q == ZL - 1) & (y < Y - 1)
    down = (q == 0) & (y > 0)

    def halo_copies(side):
        edge, slot = (y + 1, 0) if side == 0 else (y - 1, ZL + 1)
        return [
            pltpu.make_async_remote_copy(
                src_ref=cot_ref, dst_ref=cots.at[slot], send_sem=h_send.at[side, k],
                recv_sem=h_recv.at[side], device_id=dev(f, edge * ZL + k),
                device_id_type=pl.DeviceIdType.MESH,
            )
            for k in range(ZL)
        ]

    @pl.when(up)
    def _():
        for copy in halo_copies(0):
            copy.start()

    @pl.when(down)
    def _():
        for copy in halo_copies(1):
            copy.start()

    gather_own(g_block, a_send, a_recv)
    sends.append(send(g_block(f), g_block(f), a_send.at[0], a_recv.at[0], zh_dev))

    def build(j):
        value = cots[j].astype(f32)
        for b in range(TAPS):
            at = j * width if isinstance(j, int) else pl.multiple_of(j * width, width)
            S[b * chans : (b + 1) * chans, pl.ds(at, width)] = shifted(value, b - 1).astype(bf16)

    build(q + 1)

    @pl.when(y == 0)
    def _():
        cots[0] = jnp.zeros_like(cot_ref)

    @pl.when(y == Y - 1)
    def _():
        cots[ZL + 1] = jnp.zeros_like(cot_ref)

    for d in range(1, ZL):
        arrived(g2_piece(f, (q - d) % ZL), p_recv.at[d])
    gather_own(g2_block, b_send, b_recv)
    for d in range(ZL):
        arrived(g2_piece(partner, (q - d) % ZL), p_recv.at[ZL + d])
    gather_other(g2_block, b_send, b_recv)

    for d in range(1, ZL):
        arrived(cots.at[(q - d) % ZL + 1], c_recv.at[d])
        build((q - d) % ZL + 1)

    @pl.when(y > 0)
    def _():
        arrived(cots.at[0], h_recv.at[0])

    @pl.when(y < Y - 1)
    def _():
        arrived(cots.at[ZL + 1], h_recv.at[1])

    build(0)
    build(ZL + 1)
    load_f.wait()

    groups = X * ZH * CORES
    cols = width // groups
    half = width // 2
    for p in range(2):
        total = None
        for a in range(TAPS):
            at = pl.multiple_of((q + 2 - a) * width + p * half, half)
            term = lax.dot_general(
                S[:, pl.ds(at, half)], F2[a * stack : (a + 1) * stack, :],
                (((0,), (0,)), ((), ())), preferred_element_type=f32,
            )
            total = term if total is None else total + term
        for k in range(groups // 2):
            g = p * (groups // 2) + k
            IGB[g % CORES, g // (ZH * CORES), (g // CORES) % ZH] = total[cols * k : cols * (k + 1)]
    sends.append(send(IGB.at[1 - core], IGR, ig_send.at[0], ig_recv.at[0], core_dev))

    arrived(g_block(partner), a_recv.at[0])
    gather_other(g_block, a_send, a_recv)
    gather_third(g2_block, b_send, b_recv)

    gather_last(g2_block, b_send, b_recv)
    for a in range(TAPS):
        at = (2 - a) * width
        dF[a * stack : (a + 1) * stack, :] = lax.dot_general(
            S[:, at : at + ZL * width], G2[...], (((1,), (1,)), ((), ())), preferred_element_type=f32
        )
    rows = TAPS * stack // Y
    scale = scale_for(dF[...])
    for k in range(Y):
        code, tail = pack(dF[rows * k : rows * (k + 1), :], scale)
        codes[k, : 2 * rows, :] = code
        codes[k, 2 * rows :, :] = tail
    for d in range(1, Y):
        sends.append(send(codes.at[(y + d) % Y], got.at[d], rs_send.at[d], rs_recv.at[d], y_peer(d)))

    gather_third(g_block, a_send, a_recv)

    arrived(IGR, ig_recv.at[0])
    for k in range(X):
        IGB[core, k] = IGB[core, k] + IGR[k]
    for d in range(1, X):
        sends.append(send(IGB.at[core, (x + d) % X], IGX.at[d], ig_send.at[d], ig_recv.at[d], x_peer(d)))

    gather_last(g_block, a_send, a_recv)
    for a in (0, 2, 1):
        total = None
        taps = jnp.dot(F2[a * stack : (a + 1) * stack, :], G[...], preferred_element_type=f32)
        for b in range(TAPS):
            term = shifted(taps[b * chans : (b + 1) * chans], 1 - b)
            total = term if total is None else total + term
        O[a] = total

    def out_copy(a):
        return pltpu.make_async_remote_copy(
            src_ref=O.at[a], dst_ref=OR.at[a // 2], send_sem=o_send.at[a // 2], recv_sem=o_recv.at[a // 2],
            device_id=dev(f, r + 1 - a), device_id_type=pl.DeviceIdType.MESH,
        )

    @pl.when(r < Y * ZL - 1)
    def _():
        out_copy(0).start()

    @pl.when(r > 0)
    def _():
        out_copy(2).start()

    piece = dF[pl.ds(pl.multiple_of(y * rows, rows), rows), :]
    for d in range(1, Y):
        arrived(got.at[d], rs_recv.at[d])
        piece = piece + unpack(got[d])
    piece = piece / jnp.sqrt(f32(Y * ZL * width))
    code, tail = pack(piece, scale_for(piece))
    FIN[y, q, : 2 * rows, :] = code
    FIN[y, q, 2 * rows :, :] = tail
    def quarter(c):
        return (q + c) % ZL

    def crosses(step, way, c):
        return step < Y // 2 or c % 2 == way

    def ring(step, way, c):
        at = (y - (step - 1)) % Y if way == 0 else (y + (step - 1)) % Y
        ref = FIN.at[at, quarter(c)]
        to = y_peer(1 if way == 0 else -1)
        sends.append(send(ref, ref, fy_send.at[way, step, c], fy_recv.at[way, step, c], to))

    def ring_arrived(step, way, c):
        at = (y - step) % Y if way == 0 else (y + step) % Y
        arrived(FIN.at[at, quarter(c)], fy_recv.at[way, step, c])

    early = list(sends)
    sends.clear()
    for way in range(2):
        ring(1, way, 0)
    for d in range(1, ZL):
        sends.append(send(FIN.at[y, q], FIN.at[y, q], fz_send.at[d], fz_recv.at[d], zl_peer(d)))

    IGS[...] = IGB[core, x]
    for d in range(1, X):
        arrived(IGX.at[d], ig_recv.at[d])
        IGS[...] = IGS[...] + IGX[d]
    sends.append(send(IGS.at[1 - zh], IGZ, ig_send.at[X], ig_recv.at[X], zh_dev))

    for c in range(1, ZL):
        arrived(FIN.at[y, quarter(c)], fz_recv.at[ZL - c])
        for way in range(2):
            ring(1, way, c)

    lane_group = lax.broadcasted_iota(jnp.int32, (rows, 128), 1) // 16

    def result(at):
        quarters = [unpack(FIN[at, k]) for k in range(ZL)]
        for t in range(8):
            half_at, j = t // 4, t % 4
            mine = (lane_group + (8 - j)) % ZL
            tile = quarters[0][:, 128 * half_at : 128 * (half_at + 1)]
            for k in range(1, ZL):
                tile = jnp.where(mine == k, quarters[k][:, 128 * half_at : 128 * (half_at + 1)], tile)
            if j:
                tile = pltpu.roll(tile, 128 - 16 * j, 1)
            fg_ref[pl.ds(pl.multiple_of(at * rows, 8), rows), 128 * t : 128 * (t + 1)] = tile

    for step in range(1, Y // 2 + 1):
        if step > 1:
            for c in range(ZL):
                for way in range(2):
                    ring_arrived(step - 1, way, c)
                    if crosses(step, way, c):
                        ring(step, way, c)
        if step == 1:
            for copy in early:
                copy.wait_send()
            result(y)
            OUT = O.at[1]

            @pl.when(r > 0)
            def _():
                arrived(OR.at[0], o_recv.at[0])
                OUT[...] = OUT[...] + OR[0]

            @pl.when(r < Y * ZL - 1)
            def _():
                arrived(OR.at[1], o_recv.at[1])
                OUT[...] = OUT[...] + OR[1]

            out_ref[...] = OUT[...].astype(bf16)
            arrived(IGZ, ig_recv.at[X])
            ig_ref[...] = (IGS[zh] + IGZ[...]).astype(bf16)
        else:
            result((y - (step - 1)) % Y)
            result((y + (step - 1)) % Y)
    for c in range(ZL):
        ring_arrived(Y // 2, c % 2, c)
    result((y + Y // 2) % Y)

    for copy in sends:
        copy.wait_send()

    @pl.when(up)
    def _():
        for copy in halo_copies(0):
            copy.wait_send()

    @pl.when(down)
    def _():
        for copy in halo_copies(1):
            copy.wait_send()

    @pl.when(r < Y * ZL - 1)
    def _():
        out_copy(0).wait_send()

    @pl.when(r > 0)
    def _():
        out_copy(2).wait_send()


def on_device(images, filters, cotangent):
    _, chans, width = images.shape
    taps, total = filters.shape[1:]
    groups = X * ZH * CORES
    cols = width // groups
    stack = TAPS * chans
    piece = taps * chans // Y
    quarter = total // ZL
    dma = pltpu.SemaphoreType.DMA
    vmem = pltpu.VMEM
    any_spec = pl.BlockSpec(memory_space=pl.ANY)
    vmem_spec = pl.BlockSpec(memory_space=pltpu.VMEM)
    code = (2 * piece + SCALE_ROWS, quarter // 2)
    output, input_grad, grad = pl.pallas_call(
        kernel,
        out_shape=(
            jax.ShapeDtypeStruct((chans, width), bf16),
            jax.ShapeDtypeStruct((cols, total), bf16),
            jax.ShapeDtypeStruct((taps * chans, total), f32),
        ),
        in_specs=[vmem_spec, any_spec, vmem_spec],
        out_specs=(vmem_spec, vmem_spec, vmem_spec),
        scratch_shapes=[
            vmem((taps * chans, total), bf16),
            vmem((total, width), bf16),
            vmem((quarter, ZL * width), bf16),
            vmem((ZL + 2, chans, width), bf16),
            vmem((stack, (ZL + 2) * width), bf16),
            vmem((taps * chans, quarter), f32),
            vmem((Y,) + code, bf16),
            vmem((Y,) + code, bf16),
            vmem((Y, ZL) + code, bf16),
            vmem((TAPS, chans, width), f32),
            vmem((2, chans, width), f32),
            vmem((CORES, X, ZH, cols, total), f32),
            vmem((X, ZH, cols, total), f32),
            vmem((X, ZH, cols, total), f32),
            vmem((ZH, cols, total), f32),
            vmem((cols, total), f32),
            dma,
            dma((15,)), dma((15,)),
            dma((15,)), dma((15,)),
            dma((2 * ZL,)), dma((2 * ZL,)),
            dma((ZL,)), dma((ZL,)),
            dma((2, ZL)), dma((2,)),
            dma((Y,)), dma((Y,)),
            dma((2,)), dma((2,)),
            dma((X + 1,)), dma((X + 1,)),
            dma((ZL,)), dma((ZL,)),
            dma((2, Y, ZL)), dma((2, Y, ZL)),
        ],
        compiler_params=pltpu.CompilerParams(
            collective_id=0, has_side_effects=True, vmem_limit_bytes=48 * 1024 * 1024
        ),
    )(images[0], jnp.transpose(filters, (1, 0, 2)).reshape(stack * TAPS, total), cotangent[0])
    grad = jnp.transpose(grad.reshape(taps, chans, total), (1, 0, 2))
    return output[None], input_grad[None], grad


def solution(mesh):
    return jax.shard_map(
        on_device,
        mesh=mesh,
        in_specs=(P("rows", "filt", None), P("filt", None, None), P("rows", "filt", None)),
        out_specs=(P("rows", "filt", None), P("rows", "filt", None), P("filt", None, None)),
        check_vma=False,
    )
```

```python
import functools

import jax
import jax.numpy as jnp
from jax import lax
from jax.experimental import pallas as pl
from jax.experimental.pallas import tpu as pltpu
from jax.sharding import PartitionSpec as P

X, ZH, CORES = 4, 2, 2
Y, ZL = 8, 4
TAPS = 3
SCALE_ROWS = 16
TOP = 200.0
f32 = jnp.float32
bf16 = jnp.bfloat16


def shifted(value, by):
    if by == 0:
        return value
    width = value.shape[1]
    column = lax.broadcasted_iota(jnp.int32, value.shape, 1)
    rolled = pltpu.roll(value, by % width, 1)
    return jnp.where(column == (0 if by == 1 else width - 1), 0.0, rolled)


def scale_for(block):
    largest = jnp.max(jnp.abs(block), axis=(0, 1), keepdims=True)
    return (TOP / jnp.maximum(largest, 1e-30)).astype(bf16).astype(f32)


def encode(value, scale):
    t = value * scale
    t2 = t * t
    t4 = t2 * t2
    t8 = t4 * t4
    t16 = t8 * t8
    return jnp.where(t < 0.0, -t16, t16).astype(bf16)


def decode(code, inverse):
    c = code.astype(f32)
    a = jnp.abs(c)
    root = lax.rsqrt(lax.rsqrt(lax.rsqrt(lax.rsqrt(jnp.maximum(a, 1e-37)))))
    root = jnp.where(a < 1e-37, 0.0, root) * inverse
    return jnp.where(c < 0.0, -root, root)


def pack(value, scale):
    lanes = value.shape[1] // 2
    flat = jnp.concatenate([value[:, :lanes], value[:, lanes:]], axis=0)
    return encode(flat, scale), jnp.broadcast_to(scale, (SCALE_ROWS, lanes)).astype(bf16)


def unpack(code):
    rows = code.shape[0] - SCALE_ROWS
    inverse = 1.0 / code[rows : rows + 1, :].astype(f32)
    flat = decode(code[:rows, :], inverse)
    return jnp.concatenate([flat[: rows // 2], flat[rows // 2 :]], axis=1)


def kernel(
    img_ref, filt_ref, cot_ref, out_ref, ig_ref, fg_ref,
    F2, G, G2, cots, S, dF, codes, got, FIN, O, OR, IGB, IGR, IGX, IGS, IGZ,
    f_sem, a_send, a_recv, b_send, b_recv, p_send, p_recv, c_send, c_recv, h_send, h_recv,
    rs_send, rs_recv, o_send, o_recv, ig_send, ig_recv, fz_send, fz_recv, fy_send, fy_recv,
):
    f, r = lax.axis_index("filt"), lax.axis_index("rows")
    x, zh, core = f // (ZH * CORES), (f // CORES) % ZH, f % CORES
    y, q = r // ZL, r % ZL
    chans, width = img_ref.shape
    part = chans // ZL
    stack = TAPS * chans

    def dev(f_to, r_to):
        return {"filt": f_to, "rows": r_to}

    def x_peer(d):
        return dev(((x + d) % X) * (ZH * CORES) + zh * CORES + core, r)

    def zl_peer(d):
        return dev(f, y * ZL + (q + d) % ZL)

    def y_peer(d):
        return dev(f, ((y + d) % Y) * ZL + q)

    partner = f + CORES - 2 * CORES * zh
    sibling = f + 1 - 2 * core
    zh_dev, core_dev = dev(partner, r), dev(sibling, r)

    sends = []

    def zh_peer(d):
        return dev(partner, y * ZL + (q + d) % ZL)

    def send(src, dst, s_sem, r_sem, to):
        copy = pltpu.make_async_remote_copy(
            src_ref=src, dst_ref=dst, send_sem=s_sem, recv_sem=r_sem,
            device_id=to, device_id_type=pl.DeviceIdType.MESH,
        )
        copy.start()
        return copy

    def arrived(dst, r_sem):
        pltpu.make_async_remote_copy(
            src_ref=dst, dst_ref=dst, send_sem=r_sem, recv_sem=r_sem,
            device_id=core_dev, device_id_type=pl.DeviceIdType.MESH,
        ).wait_recv()

    def g_block(k):
        return G.at[pl.ds(pl.multiple_of(k * chans, chans), chans), :]

    load_img = pltpu.make_async_copy(img_ref, g_block(f), f_sem.at[0])
    load_cot = pltpu.make_async_copy(cot_ref, cots.at[q + 1], f_sem.at[1])
    load_f = pltpu.make_async_copy(filt_ref, F2, f_sem.at[2])
    for load in (load_img, load_cot, load_f):
        load.start()

    barrier = pltpu.get_barrier_semaphore()

    def greet(to):
        pl.semaphore_signal(barrier, inc=1, device_id=to, device_id_type=pl.DeviceIdType.MESH)

    fixed = [x_peer(d) for d in range(1, X)] + [zl_peer(d) for d in range(1, ZL)]
    fixed += [y_peer(d) for d in range(1, Y)] + [core_dev] + [zh_peer(d) for d in range(ZL)]
    for to in fixed:
        greet(to)

    below, above = (y > 0) & (q == 0), (y < Y - 1) & (q == ZL - 1)

    @pl.when(below)
    def _():
        greet(dev(f, r - 1))

    @pl.when(above)
    def _():
        greet(dev(f, r + 1))

    def g2_rows(k, to=q):
        at = 8 * (k // 8) + (to + 4 * (k % 2) + (k % 8) // 2) % 8
        return pl.ds(pl.multiple_of(at * part, part), part)

    def g2_block(k):
        return G2.at[g2_rows(k), :]

    def g2_piece(k, row, to=q):
        return G2.at[g2_rows(k, to), pl.ds(pl.multiple_of(row * width, width), width)]

    load_img.wait()
    load_cot.wait()
    g2_piece(f, q)[...] = G[pl.ds(pl.multiple_of(f * chans + q * part, part), part), :]
    others = jnp.where(below, 1, 0) + jnp.where(above, 1, 0)
    pl.semaphore_wait(barrier, len(fixed) + others)

    for d in list(range(ZL, 2 * ZL)) + list(range(1, ZL)):
        to = (q + d) % ZL
        sends.append(send(
            G.at[pl.ds(pl.multiple_of(f * chans + to * part, part), part), :], g2_piece(f, q, to),
            p_send.at[d], p_recv.at[d], zl_peer(d) if d < ZL else zh_peer(d),
        ))

    def gather_own(block, s_sem, r_sem):
        mine = block(f)
        for d in range(1, X):
            sends.append(send(mine, mine, s_sem.at[d], r_sem.at[d], x_peer(d)))
        sends.append(send(mine, mine, s_sem.at[4], r_sem.at[4], core_dev))

    def gather_other(block, s_sem, r_sem):
        other = block(partner)
        for d in range(1, X):
            sends.append(send(other, other, s_sem.at[4 + d], r_sem.at[4 + d], x_peer(d)))
        sends.append(send(other, other, s_sem.at[8], r_sem.at[8], core_dev))

    def gather_third(block, s_sem, r_sem):
        for d in range(1, X):
            x_from = ((x - d) % X) * (ZH * CORES) + core
            for second in range(2):
                k = x_from + CORES * (zh if second == 0 else 1 - zh)
                theirs = block(k)
                arrived(theirs, r_sem.at[d + 4 * second])
                at = 9 + 2 * (d - 1) + second
                sends.append(send(theirs, theirs, s_sem.at[at], r_sem.at[at], core_dev))

    def gather_last(block, s_sem, r_sem):
        base = 1 - core
        arrived(block(sibling), r_sem.at[4])
        arrived(block(partner + 1 - 2 * core), r_sem.at[8])
        for d in range(1, X):
            x_from = ((x - d) % X) * (ZH * CORES) + base
            for second in range(2):
                k = x_from + CORES * (zh if second == 0 else 1 - zh)
                arrived(block(k), r_sem.at[9 + 2 * (d - 1) + second])

    for d in range(1, ZL):
        mine = cots.at[q + 1]
        sends.append(send(mine, mine, c_send.at[d], c_recv.at[d], zl_peer(d)))

    def halo_copy(side):
        source, slot, step = (ZL, 0, 1) if side == 0 else (1, ZL + 1, -1)
        return pltpu.make_async_remote_copy(
            src_ref=cots.at[source], dst_ref=cots.at[slot], send_sem=h_send.at[side],
            recv_sem=h_recv.at[side], device_id=y_peer(step), device_id_type=pl.DeviceIdType.MESH,
        )

    def build(j):
        value = cots[j].astype(f32)
        for b in range(TAPS):
            at = j * width if isinstance(j, int) else pl.multiple_of(j * width, width)
            S[b * chans : (b + 1) * chans, pl.ds(at, width)] = shifted(value, b - 1).astype(bf16)

    build(q + 1)

    @pl.when(y == 0)
    def _():
        cots[0] = jnp.zeros_like(cot_ref)

    @pl.when(y == Y - 1)
    def _():
        cots[ZL + 1] = jnp.zeros_like(cot_ref)

    for d in range(1, ZL):
        arrived(g2_piece(f, (q - d) % ZL), p_recv.at[d])
    gather_own(g2_block, b_send, b_recv)
    sends.append(send(g_block(f), g_block(f), a_send.at[0], a_recv.at[0], zh_dev))
    for d in range(ZL):
        arrived(g2_piece(partner, (q - d) % ZL), p_recv.at[ZL + d])
    gather_other(g2_block, b_send, b_recv)
    gather_own(g_block, a_send, a_recv)

    for d in range(1, ZL):
        arrived(cots.at[(q - d) % ZL + 1], c_recv.at[d])

    @pl.when(y < Y - 1)
    def _():
        halo_copy(0).start()

    @pl.when(y > 0)
    def _():
        halo_copy(1).start()

    for d in range(1, ZL):
        build((q - d) % ZL + 1)

    gather_third(g2_block, b_send, b_recv)

    gather_last(g2_block, b_send, b_recv)

    def grad_term(a, first, last):
        at = (2 - a + first) * width
        return lax.dot_general(
            S[:, at : at + (last - first) * width], G2[:, first * width : last * width],
            (((1,), (1,)), ((), ())), preferred_element_type=f32,
        )

    dF[stack : 2 * stack, :] = grad_term(1, 0, ZL)
    dF[:stack, :] = grad_term(0, 0, ZL - 1)
    dF[2 * stack :, :] = grad_term(2, 1, ZL)

    @pl.when(y > 0)
    def _():
        arrived(cots.at[0], h_recv.at[0])

    @pl.when(y < Y - 1)
    def _():
        arrived(cots.at[ZL + 1], h_recv.at[1])

    build(0)
    build(ZL + 1)

    dF[:stack, :] += grad_term(0, ZL - 1, ZL)
    dF[2 * stack :, :] += grad_term(2, 0, 1)
    rows = TAPS * stack // Y
    scale = scale_for(dF[...])
    for k in range(Y):
        code, tail = pack(dF[rows * k : rows * (k + 1), :], scale)
        codes[k, : 2 * rows, :] = code
        codes[k, 2 * rows :, :] = tail
    for d in range(1, Y):
        sends.append(send(codes.at[(y + d) % Y], got.at[d], rs_send.at[d], rs_recv.at[d], y_peer(d)))

    load_f.wait()
    groups = X * ZH * CORES
    cols = width // groups
    half = width // 2
    for p in range(2):
        total = None
        for a in range(TAPS):
            at = pl.multiple_of((q + 2 - a) * width + p * half, half)
            term = lax.dot_general(
                S[:, pl.ds(at, half)], F2[a * stack : (a + 1) * stack, :],
                (((0,), (0,)), ((), ())), preferred_element_type=f32,
            )
            total = term if total is None else total + term
        for k in range(groups // 2):
            g = p * (groups // 2) + k
            IGB[g % CORES, g // (ZH * CORES), (g // CORES) % ZH] = total[cols * k : cols * (k + 1)]
    sends.append(send(IGB.at[1 - core], IGR, ig_send.at[0], ig_recv.at[0], core_dev))

    arrived(g_block(partner), a_recv.at[0])
    gather_other(g_block, a_send, a_recv)

    arrived(IGR, ig_recv.at[0])
    for k in range(X):
        IGB[core, k] = IGB[core, k] + IGR[k]
    for d in range(1, X):
        sends.append(send(IGB.at[core, (x + d) % X], IGX.at[d], ig_send.at[d], ig_recv.at[d], x_peer(d)))

    gather_third(g_block, a_send, a_recv)

    piece = dF[pl.ds(pl.multiple_of(y * rows, rows), rows), :]
    for d in range(1, Y):
        arrived(got.at[d], rs_recv.at[d])
        piece = piece + unpack(got[d])
    piece = piece / jnp.sqrt(f32(Y * ZL * width))
    code, tail = pack(piece, scale_for(piece))
    FIN[y, q, : 2 * rows, :] = code
    FIN[y, q, 2 * rows :, :] = tail
    def quarter(c):
        return (q + c) % ZL

    def crosses(step, way, c):
        return step < Y // 2 or c % 2 == way

    def ring(step, way, c):
        at = (y - (step - 1)) % Y if way == 0 else (y + (step - 1)) % Y
        ref = FIN.at[at, quarter(c)]
        to = y_peer(1 if way == 0 else -1)
        sends.append(send(ref, ref, fy_send.at[way, step, c], fy_recv.at[way, step, c], to))

    def ring_arrived(step, way, c):
        at = (y - step) % Y if way == 0 else (y + step) % Y
        arrived(FIN.at[at, quarter(c)], fy_recv.at[way, step, c])

    early = list(sends)
    sends.clear()
    for way in range(2):
        ring(1, way, 0)
    for d in range(1, ZL):
        sends.append(send(FIN.at[y, q], FIN.at[y, q], fz_send.at[d], fz_recv.at[d], zl_peer(d)))

    gather_last(g_block, a_send, a_recv)
    for a in (0, 2, 1):
        total = None
        taps = jnp.dot(F2[a * stack : (a + 1) * stack, :], G[...], preferred_element_type=f32)
        for b in range(TAPS):
            term = shifted(taps[b * chans : (b + 1) * chans], 1 - b)
            total = term if total is None else total + term
        O[a] = total

    def out_copy(a):
        return pltpu.make_async_remote_copy(
            src_ref=O.at[a], dst_ref=OR.at[a // 2], send_sem=o_send.at[a // 2], recv_sem=o_recv.at[a // 2],
            device_id=dev(f, r + 1 - a), device_id_type=pl.DeviceIdType.MESH,
        )

    @pl.when(r < Y * ZL - 1)
    def _():
        out_copy(0).start()

    @pl.when(r > 0)
    def _():
        out_copy(2).start()

    for c in range(1, ZL):
        arrived(FIN.at[y, quarter(c)], fz_recv.at[ZL - c])
        for way in range(2):
            ring(1, way, c)

    lane_group = lax.broadcasted_iota(jnp.int32, (rows, 128), 1) // 16

    def result(at):
        quarters = [unpack(FIN[at, k]) for k in range(ZL)]
        for t in range(8):
            half_at, j = t // 4, t % 4
            mine = (lane_group + (8 - j)) % ZL
            tile = quarters[0][:, 128 * half_at : 128 * (half_at + 1)]
            for k in range(1, ZL):
                tile = jnp.where(mine == k, quarters[k][:, 128 * half_at : 128 * (half_at + 1)], tile)
            if j:
                tile = pltpu.roll(tile, 128 - 16 * j, 1)
            fg_ref[pl.ds(pl.multiple_of(at * rows, 8), rows), 128 * t : 128 * (t + 1)] = tile

    for step in range(1, Y // 2 + 1):
        if step > 1:
            for c in range(ZL):
                for way in range(2):
                    ring_arrived(step - 1, way, c)
                    if crosses(step, way, c):
                        ring(step, way, c)
        if step == 1:
            for copy in early:
                copy.wait_send()
            result(y)
            IGS[...] = IGB[core, x]
            for d in range(1, X):
                arrived(IGX.at[d], ig_recv.at[d])
                IGS[...] = IGS[...] + IGX[d]
            sends.append(send(IGS.at[1 - zh], IGZ, ig_send.at[X], ig_recv.at[X], zh_dev))
        else:
            result((y - (step - 1)) % Y)
            result((y + (step - 1)) % Y)
    for c in range(ZL):
        ring_arrived(Y // 2, c % 2, c)
    result((y + Y // 2) % Y)

    OUT = O.at[1]

    @pl.when(r > 0)
    def _():
        arrived(OR.at[0], o_recv.at[0])
        OUT[...] = OUT[...] + OR[0]

    @pl.when(r < Y * ZL - 1)
    def _():
        arrived(OR.at[1], o_recv.at[1])
        OUT[...] = OUT[...] + OR[1]

    out_ref[...] = OUT[...].astype(bf16)
    arrived(IGZ, ig_recv.at[X])
    ig_ref[...] = (IGS[zh] + IGZ[...]).astype(bf16)

    for copy in sends:
        copy.wait_send()

    @pl.when(y < Y - 1)
    def _():
        halo_copy(0).wait_send()

    @pl.when(y > 0)
    def _():
        halo_copy(1).wait_send()

    @pl.when(r < Y * ZL - 1)
    def _():
        out_copy(0).wait_send()

    @pl.when(r > 0)
    def _():
        out_copy(2).wait_send()


def on_device(images, filters, cotangent):
    _, chans, width = images.shape
    taps, total = filters.shape[1:]
    groups = X * ZH * CORES
    cols = width // groups
    stack = TAPS * chans
    piece = taps * chans // Y
    quarter = total // ZL
    dma = pltpu.SemaphoreType.DMA
    vmem = pltpu.VMEM
    hbm_spec = pl.BlockSpec(memory_space=pltpu.HBM)
    vmem_spec = pl.BlockSpec(memory_space=pltpu.VMEM)
    code = (2 * piece + SCALE_ROWS, quarter // 2)
    output, input_grad, grad = pl.pallas_call(
        kernel,
        out_shape=(
            jax.ShapeDtypeStruct((chans, width), bf16),
            jax.ShapeDtypeStruct((cols, total), bf16),
            jax.ShapeDtypeStruct((taps * chans, total), f32),
        ),
        in_specs=[hbm_spec, hbm_spec, hbm_spec],
        out_specs=(vmem_spec, vmem_spec, vmem_spec),
        scratch_shapes=[
            vmem((taps * chans, total), bf16),
            vmem((total, width), bf16),
            vmem((quarter, ZL * width), bf16),
            vmem((ZL + 2, chans, width), bf16),
            vmem((stack, (ZL + 2) * width), bf16),
            vmem((taps * chans, quarter), f32),
            vmem((Y,) + code, bf16),
            vmem((Y,) + code, bf16),
            vmem((Y, ZL) + code, bf16),
            vmem((TAPS, chans, width), f32),
            vmem((2, chans, width), f32),
            vmem((CORES, X, ZH, cols, total), f32),
            vmem((X, ZH, cols, total), f32),
            vmem((X, ZH, cols, total), f32),
            vmem((ZH, cols, total), f32),
            vmem((cols, total), f32),
            dma((3,)),
            dma((15,)), dma((15,)),
            dma((15,)), dma((15,)),
            dma((2 * ZL,)), dma((2 * ZL,)),
            dma((ZL,)), dma((ZL,)),
            dma((2,)), dma((2,)),
            dma((Y,)), dma((Y,)),
            dma((2,)), dma((2,)),
            dma((X + 1,)), dma((X + 1,)),
            dma((ZL,)), dma((ZL,)),
            dma((2, Y, ZL)), dma((2, Y, ZL)),
        ],
        compiler_params=pltpu.CompilerParams(
            collective_id=0, has_side_effects=True, vmem_limit_bytes=48 * 1024 * 1024
        ),
    )(images[0], jnp.transpose(filters, (1, 0, 2)).reshape(stack * TAPS, total), cotangent[0])
    grad = jnp.transpose(grad.reshape(taps, chans, total), (1, 0, 2))
    return output[None], input_grad[None], grad


def solution(mesh):
    return jax.shard_map(
        on_device,
        mesh=mesh,
        in_specs=(P("rows", "filt", None), P("filt", None, None), P("rows", "filt", None)),
        out_specs=(P("rows", "filt", None), P("rows", "filt", None), P("filt", None, None)),
        check_vma=False,
    )
```

```python
import functools

import jax
import jax.numpy as jnp
from jax import lax
from jax.experimental import pallas as pl
from jax.experimental.pallas import tpu as pltpu
from jax.sharding import PartitionSpec as P

X, ZH, CORES = 4, 2, 2
Y, ZL = 8, 4
TAPS = 3
SCALE_ROWS = 16
TOP = 200.0
f32 = jnp.float32
bf16 = jnp.bfloat16


def shifted(value, by):
    if by == 0:
        return value
    width = value.shape[1]
    column = lax.broadcasted_iota(jnp.int32, value.shape, 1)
    rolled = pltpu.roll(value, by % width, 1)
    return jnp.where(column == (0 if by == 1 else width - 1), 0.0, rolled)


def scale_for(block):
    largest = jnp.max(jnp.abs(block), axis=(0, 1), keepdims=True)
    return (TOP / jnp.maximum(largest, 1e-30)).astype(bf16).astype(f32)


def encode(value, scale):
    t = value * scale
    t2 = t * t
    t4 = t2 * t2
    t8 = t4 * t4
    t16 = t8 * t8
    return jnp.where(t < 0.0, -t16, t16).astype(bf16)


def decode(code, inverse):
    c = code.astype(f32)
    a = jnp.abs(c)
    root = lax.rsqrt(lax.rsqrt(lax.rsqrt(lax.rsqrt(jnp.maximum(a, 1e-37)))))
    root = jnp.where(a < 1e-37, 0.0, root) * inverse
    return jnp.where(c < 0.0, -root, root)


def pack(value, scale):
    lanes = value.shape[1] // 2
    flat = jnp.concatenate([value[:, :lanes], value[:, lanes:]], axis=0)
    return encode(flat, scale), jnp.broadcast_to(scale, (SCALE_ROWS, lanes)).astype(bf16)


def unpack(code):
    rows = code.shape[0] - SCALE_ROWS
    inverse = 1.0 / code[rows : rows + 1, :].astype(f32)
    flat = decode(code[:rows, :], inverse)
    return jnp.concatenate([flat[: rows // 2], flat[rows // 2 :]], axis=1)


def kernel(
    rows_ref, filt_ref, out_ref, ig_ref, fg_ref,
    F2, G, G2, cots, S, dF, codes, got, FIN, O, OR, IGB, IGR, IGX, IGS, IGZ,
    f_sem, a_send, a_recv, b_send, b_recv, p_send, p_recv, c_send, c_recv, h_send, h_recv,
    rs_send, rs_recv, o_send, o_recv, ig_send, ig_recv, fz_send, fz_recv, fy_send, fy_recv,
):
    f, r = lax.axis_index("filt"), lax.axis_index("rows")
    x, zh, core = f // (ZH * CORES), (f // CORES) % ZH, f % CORES
    y, q = r // ZL, r % ZL
    _, chans, width = rows_ref.shape
    part = chans // ZL
    stack = TAPS * chans

    def dev(f_to, r_to):
        return {"filt": f_to, "rows": r_to}

    def x_peer(d):
        return dev(((x + d) % X) * (ZH * CORES) + zh * CORES + core, r)

    def zl_peer(d):
        return dev(f, y * ZL + (q + d) % ZL)

    def y_peer(d):
        return dev(f, ((y + d) % Y) * ZL + q)

    partner = f + CORES - 2 * CORES * zh
    sibling = f + 1 - 2 * core
    zh_dev, core_dev = dev(partner, r), dev(sibling, r)

    sends = []

    def zh_peer(d):
        return dev(partner, y * ZL + (q + d) % ZL)

    def send(src, dst, s_sem, r_sem, to):
        copy = pltpu.make_async_remote_copy(
            src_ref=src, dst_ref=dst, send_sem=s_sem, recv_sem=r_sem,
            device_id=to, device_id_type=pl.DeviceIdType.MESH,
        )
        copy.start()
        return copy

    def arrived(dst, r_sem):
        pltpu.make_async_remote_copy(
            src_ref=dst, dst_ref=dst, send_sem=r_sem, recv_sem=r_sem,
            device_id=core_dev, device_id_type=pl.DeviceIdType.MESH,
        ).wait_recv()

    def g_block(k):
        return G.at[pl.ds(pl.multiple_of(k * chans, chans), chans), :]

    load_img = pltpu.make_async_copy(rows_ref.at[0], g_block(f), f_sem.at[0])
    load_cot = pltpu.make_async_copy(rows_ref.at[1], cots.at[q + 1], f_sem.at[1])
    load_f = pltpu.make_async_copy(filt_ref, F2, f_sem.at[2])
    for load in (load_img, load_cot, load_f):
        load.start()

    barrier = pltpu.get_barrier_semaphore()

    def greet(to):
        pl.semaphore_signal(barrier, inc=1, device_id=to, device_id_type=pl.DeviceIdType.MESH)

    fixed = [x_peer(d) for d in range(1, X)] + [zl_peer(d) for d in range(1, ZL)]
    fixed += [y_peer(d) for d in range(1, Y)] + [core_dev] + [zh_peer(d) for d in range(ZL)]
    for to in fixed:
        greet(to)

    below, above = (y > 0) & (q == 0), (y < Y - 1) & (q == ZL - 1)

    @pl.when(below)
    def _():
        greet(dev(f, r - 1))

    @pl.when(above)
    def _():
        greet(dev(f, r + 1))

    def g2_rows(k, to=q):
        at = 8 * (k // 8) + (to + 4 * (k % 2) + (k % 8) // 2) % 8
        return pl.ds(pl.multiple_of(at * part, part), part)

    def g2_block(k):
        return G2.at[g2_rows(k), :]

    def g2_piece(k, row, to=q):
        return G2.at[g2_rows(k, to), pl.ds(pl.multiple_of(row * width, width), width)]

    load_img.wait()
    load_cot.wait()
    g2_piece(f, q)[...] = G[pl.ds(pl.multiple_of(f * chans + q * part, part), part), :]
    others = jnp.where(below, 1, 0) + jnp.where(above, 1, 0)
    pl.semaphore_wait(barrier, len(fixed) + others)

    for d in list(range(ZL, 2 * ZL)) + list(range(1, ZL)):
        to = (q + d) % ZL
        sends.append(send(
            G.at[pl.ds(pl.multiple_of(f * chans + to * part, part), part), :], g2_piece(f, q, to),
            p_send.at[d], p_recv.at[d], zl_peer(d) if d < ZL else zh_peer(d),
        ))

    def gather_own(block, s_sem, r_sem):
        mine = block(f)
        for d in range(1, X):
            sends.append(send(mine, mine, s_sem.at[d], r_sem.at[d], x_peer(d)))
        sends.append(send(mine, mine, s_sem.at[4], r_sem.at[4], core_dev))

    def gather_other(block, s_sem, r_sem):
        other = block(partner)
        for d in range(1, X):
            sends.append(send(other, other, s_sem.at[4 + d], r_sem.at[4 + d], x_peer(d)))
        sends.append(send(other, other, s_sem.at[8], r_sem.at[8], core_dev))

    def gather_third(block, s_sem, r_sem):
        for d in range(1, X):
            x_from = ((x - d) % X) * (ZH * CORES) + core
            for second in range(2):
                k = x_from + CORES * (zh if second == 0 else 1 - zh)
                theirs = block(k)
                arrived(theirs, r_sem.at[d + 4 * second])
                at = 9 + 2 * (d - 1) + second
                sends.append(send(theirs, theirs, s_sem.at[at], r_sem.at[at], core_dev))

    def gather_last(block, s_sem, r_sem):
        base = 1 - core
        arrived(block(sibling), r_sem.at[4])
        arrived(block(partner + 1 - 2 * core), r_sem.at[8])
        for d in range(1, X):
            x_from = ((x - d) % X) * (ZH * CORES) + base
            for second in range(2):
                k = x_from + CORES * (zh if second == 0 else 1 - zh)
                arrived(block(k), r_sem.at[9 + 2 * (d - 1) + second])

    for d in range(1, ZL):
        mine = cots.at[q + 1]
        sends.append(send(mine, mine, c_send.at[d], c_recv.at[d], zl_peer(d)))

    gather_own(g_block, a_send, a_recv)

    def halo_copy(side):
        source, slot, step = (ZL, 0, 1) if side == 0 else (1, ZL + 1, -1)
        return pltpu.make_async_remote_copy(
            src_ref=cots.at[source], dst_ref=cots.at[slot], send_sem=h_send.at[side],
            recv_sem=h_recv.at[side], device_id=y_peer(step), device_id_type=pl.DeviceIdType.MESH,
        )

    def build(j):
        value = cots[j].astype(f32)
        for b in range(TAPS):
            at = j * width if isinstance(j, int) else pl.multiple_of(j * width, width)
            S[b * chans : (b + 1) * chans, pl.ds(at, width)] = shifted(value, b - 1).astype(bf16)

    build(q + 1)

    @pl.when(y == 0)
    def _():
        cots[0] = jnp.zeros((chans, width), bf16)

    @pl.when(y == Y - 1)
    def _():
        cots[ZL + 1] = jnp.zeros((chans, width), bf16)

    for d in range(1, ZL):
        arrived(g2_piece(f, (q - d) % ZL), p_recv.at[d])
    gather_own(g2_block, b_send, b_recv)
    sends.append(send(g_block(f), g_block(f), a_send.at[0], a_recv.at[0], zh_dev))
    for d in range(ZL):
        arrived(g2_piece(partner, (q - d) % ZL), p_recv.at[ZL + d])
    gather_other(g2_block, b_send, b_recv)

    for d in range(1, ZL):
        arrived(cots.at[(q - d) % ZL + 1], c_recv.at[d])

    @pl.when(y < Y - 1)
    def _():
        halo_copy(0).start()

    @pl.when(y > 0)
    def _():
        halo_copy(1).start()

    for d in range(1, ZL):
        build((q - d) % ZL + 1)

    gather_third(g2_block, b_send, b_recv)

    gather_last(g2_block, b_send, b_recv)

    arrived(g_block(partner), a_recv.at[0])
    gather_other(g_block, a_send, a_recv)

    def grad_term(a, first, last):
        at = (2 - a + first) * width
        return lax.dot_general(
            S[:, at : at + (last - first) * width], G2[:, first * width : last * width],
            (((1,), (1,)), ((), ())), preferred_element_type=f32,
        )

    dF[stack : 2 * stack, :] = grad_term(1, 0, ZL)
    dF[:stack, :] = grad_term(0, 0, ZL - 1)
    dF[2 * stack :, :] = grad_term(2, 1, ZL)

    @pl.when(y > 0)
    def _():
        arrived(cots.at[0], h_recv.at[0])

    @pl.when(y < Y - 1)
    def _():
        arrived(cots.at[ZL + 1], h_recv.at[1])

    build(0)
    build(ZL + 1)

    dF[:stack, :] += grad_term(0, ZL - 1, ZL)
    dF[2 * stack :, :] += grad_term(2, 0, 1)
    rows = TAPS * stack // Y
    scale = scale_for(dF[...])
    for k in range(Y):
        code, tail = pack(dF[rows * k : rows * (k + 1), :], scale)
        codes[k, : 2 * rows, :] = code
        codes[k, 2 * rows :, :] = tail
    for d in range(1, Y):
        sends.append(send(codes.at[(y + d) % Y], got.at[d], rs_send.at[d], rs_recv.at[d], y_peer(d)))

    load_f.wait()
    groups = X * ZH * CORES
    cols = width // groups
    half = width // 2
    for p in range(2):
        total = None
        for a in range(TAPS):
            at = pl.multiple_of((q + 2 - a) * width + p * half, half)
            term = lax.dot_general(
                S[:, pl.ds(at, half)], F2[a * stack : (a + 1) * stack, :],
                (((0,), (0,)), ((), ())), preferred_element_type=f32,
            )
            total = term if total is None else total + term
        for k in range(groups // 2):
            g = p * (groups // 2) + k
            IGB[g % CORES, g // (ZH * CORES), (g // CORES) % ZH] = total[cols * k : cols * (k + 1)]
    sends.append(send(IGB.at[1 - core], IGR, ig_send.at[0], ig_recv.at[0], core_dev))


    gather_third(g_block, a_send, a_recv)

    gather_last(g_block, a_send, a_recv)
    for a in (0, 2, 1):
        total = None
        taps = jnp.dot(F2[a * stack : (a + 1) * stack, :], G[...], preferred_element_type=f32)
        for b in range(TAPS):
            term = shifted(taps[b * chans : (b + 1) * chans], 1 - b)
            total = term if total is None else total + term
        O[a] = total

    def out_copy(a):
        return pltpu.make_async_remote_copy(
            src_ref=O.at[a], dst_ref=OR.at[a // 2], send_sem=o_send.at[a // 2], recv_sem=o_recv.at[a // 2],
            device_id=dev(f, r + 1 - a), device_id_type=pl.DeviceIdType.MESH,
        )

    arrived(IGR, ig_recv.at[0])
    for k in range(X):
        IGB[core, k] = IGB[core, k] + IGR[k]
    for d in range(1, X):
        sends.append(send(IGB.at[core, (x + d) % X], IGX.at[d], ig_send.at[d], ig_recv.at[d], x_peer(d)))


    piece = dF[pl.ds(pl.multiple_of(y * rows, rows), rows), :]
    for d in range(1, Y):
        arrived(got.at[d], rs_recv.at[d])
        piece = piece + unpack(got[d])
    piece = piece / jnp.sqrt(f32(Y * ZL * width))
    code, tail = pack(piece, scale_for(piece))
    FIN[y, q, : 2 * rows, :] = code
    FIN[y, q, 2 * rows :, :] = tail
    def quarter(c):
        return (q + c) % ZL

    def crosses(step, way, c):
        return step < Y // 2 or c % 2 == way

    def ring(step, way, c):
        at = (y - (step - 1)) % Y if way == 0 else (y + (step - 1)) % Y
        ref = FIN.at[at, quarter(c)]
        to = y_peer(1 if way == 0 else -1)
        sends.append(send(ref, ref, fy_send.at[way, step, c], fy_recv.at[way, step, c], to))

    def ring_arrived(step, way, c):
        at = (y - step) % Y if way == 0 else (y + step) % Y
        arrived(FIN.at[at, quarter(c)], fy_recv.at[way, step, c])

    def pass_on(step, c):
        for way in range(2):
            if crosses(step, way, c):
                ring_arrived(step, way, c)
                if step < Y // 2 and crosses(step + 1, way, c):
                    ring(step + 1, way, c)

    early = list(sends)
    sends.clear()
    for way in range(2):
        ring(1, way, 0)
    for d in range(1, ZL):
        sends.append(send(FIN.at[y, q], FIN.at[y, q], fz_send.at[d], fz_recv.at[d], zl_peer(d)))

    pass_on(1, 0)
    for c in range(1, ZL):
        arrived(FIN.at[y, quarter(c)], fz_recv.at[ZL - c])
        for way in range(2):
            ring(1, way, c)

    @pl.when(r < Y * ZL - 1)
    def _():
        out_copy(0).start()

    @pl.when(r > 0)
    def _():
        out_copy(2).start()

    lane_group = lax.broadcasted_iota(jnp.int32, (rows, 128), 1) // 16

    def result(at):
        quarters = [unpack(FIN[at, k]) for k in range(ZL)]
        for t in range(8):
            half_at, j = t // 4, t % 4
            mine = (lane_group + (8 - j)) % ZL
            tile = quarters[0][:, 128 * half_at : 128 * (half_at + 1)]
            for k in range(1, ZL):
                tile = jnp.where(mine == k, quarters[k][:, 128 * half_at : 128 * (half_at + 1)], tile)
            if j:
                tile = pltpu.roll(tile, 128 - 16 * j, 1)
            fg_ref[pl.ds(pl.multiple_of(at * rows, 8), rows), 128 * t : 128 * (t + 1)] = tile

    result(y)
    for step in range(1, Y // 2 + 1):
        for c in range(1, ZL):
            pass_on(step, c)
        if step < Y // 2:
            pass_on(step + 1, 0)
            result((y - step) % Y)
            result((y + step) % Y)
        if step == 1:
            IGS[...] = IGB[core, x]
            for d in range(1, X):
                arrived(IGX.at[d], ig_recv.at[d])
                IGS[...] = IGS[...] + IGX[d]
            sends.append(send(IGS.at[1 - zh], IGZ, ig_send.at[X], ig_recv.at[X], zh_dev))
            for copy in early:
                copy.wait_send()
    result((y + Y // 2) % Y)

    OUT = O.at[1]

    @pl.when(r > 0)
    def _():
        arrived(OR.at[0], o_recv.at[0])
        OUT[...] = OUT[...] + OR[0]

    @pl.when(r < Y * ZL - 1)
    def _():
        arrived(OR.at[1], o_recv.at[1])
        OUT[...] = OUT[...] + OR[1]

    out_ref[...] = OUT[...].astype(bf16)
    arrived(IGZ, ig_recv.at[X])
    ig_ref[...] = (IGS[zh] + IGZ[...]).astype(bf16)

    for copy in sends:
        copy.wait_send()

    @pl.when(y < Y - 1)
    def _():
        halo_copy(0).wait_send()

    @pl.when(y > 0)
    def _():
        halo_copy(1).wait_send()

    @pl.when(r < Y * ZL - 1)
    def _():
        out_copy(0).wait_send()

    @pl.when(r > 0)
    def _():
        out_copy(2).wait_send()


def on_device(images, filters, cotangent):
    _, chans, width = images.shape
    taps, total = filters.shape[1:]
    groups = X * ZH * CORES
    cols = width // groups
    stack = TAPS * chans
    piece = taps * chans // Y
    quarter = total // ZL
    dma = pltpu.SemaphoreType.DMA
    vmem = pltpu.VMEM
    hbm_spec = pl.BlockSpec(memory_space=pltpu.HBM)
    vmem_spec = pl.BlockSpec(memory_space=pltpu.VMEM)
    code = (2 * piece + SCALE_ROWS, quarter // 2)
    output, input_grad, grad = pl.pallas_call(
        kernel,
        out_shape=(
            jax.ShapeDtypeStruct((chans, width), bf16),
            jax.ShapeDtypeStruct((cols, total), bf16),
            jax.ShapeDtypeStruct((taps * chans, total), f32),
        ),
        in_specs=[hbm_spec, hbm_spec],
        out_specs=(vmem_spec, vmem_spec, vmem_spec),
        scratch_shapes=[
            vmem((taps * chans, total), bf16),
            vmem((total, width), bf16),
            vmem((quarter, ZL * width), bf16),
            vmem((ZL + 2, chans, width), bf16),
            vmem((stack, (ZL + 2) * width), bf16),
            vmem((taps * chans, quarter), f32),
            vmem((Y,) + code, bf16),
            vmem((Y,) + code, bf16),
            vmem((Y, ZL) + code, bf16),
            vmem((TAPS, chans, width), f32),
            vmem((2, chans, width), f32),
            vmem((CORES, X, ZH, cols, total), f32),
            vmem((X, ZH, cols, total), f32),
            vmem((X, ZH, cols, total), f32),
            vmem((ZH, cols, total), f32),
            vmem((cols, total), f32),
            dma((3,)),
            dma((15,)), dma((15,)),
            dma((15,)), dma((15,)),
            dma((2 * ZL,)), dma((2 * ZL,)),
            dma((ZL,)), dma((ZL,)),
            dma((2,)), dma((2,)),
            dma((Y,)), dma((Y,)),
            dma((2,)), dma((2,)),
            dma((X + 1,)), dma((X + 1,)),
            dma((ZL,)), dma((ZL,)),
            dma((2, Y, ZL)), dma((2, Y, ZL)),
        ],
        compiler_params=pltpu.CompilerParams(
            collective_id=0, has_side_effects=True, vmem_limit_bytes=48 * 1024 * 1024
        ),
    )(jnp.concatenate([images, cotangent]), jnp.transpose(filters, (1, 0, 2)).reshape(stack * TAPS, total))
    grad = jnp.transpose(grad.reshape(taps, chans, total), (1, 0, 2))
    return output[None], input_grad[None], grad


def solution(mesh):
    return jax.shard_map(
        on_device,
        mesh=mesh,
        in_specs=(P("rows", "filt", None), P("filt", None, None), P("rows", "filt", None)),
        out_specs=(P("rows", "filt", None), P("rows", "filt", None), P("filt", None, None)),
        check_vma=False,
    )
```

```python
import functools

import jax
import jax.numpy as jnp
from jax import lax
from jax.experimental import pallas as pl
from jax.experimental.pallas import tpu as pltpu
from jax.sharding import PartitionSpec as P

X, ZH, CORES = 4, 2, 2
Y, ZL = 8, 4
TAPS = 3
SCALE_ROWS = 16
TOP = 200.0
f32 = jnp.float32
bf16 = jnp.bfloat16


def shifted(value, by):
    if by == 0:
        return value
    width = value.shape[1]
    column = lax.broadcasted_iota(jnp.int32, value.shape, 1)
    rolled = pltpu.roll(value, by % width, 1)
    return jnp.where(column == (0 if by == 1 else width - 1), 0.0, rolled)


def scale_for(block):
    largest = jnp.max(jnp.abs(block), axis=(0, 1), keepdims=True)
    return (TOP / jnp.maximum(largest, 1e-30)).astype(bf16).astype(f32)


def encode(value, scale):
    t = value * scale
    t2 = t * t
    t4 = t2 * t2
    t8 = t4 * t4
    t16 = t8 * t8
    return jnp.where(t < 0.0, -t16, t16).astype(bf16)


def decode(code, inverse):
    c = code.astype(f32)
    a = jnp.abs(c)
    root = lax.rsqrt(lax.rsqrt(lax.rsqrt(lax.rsqrt(jnp.maximum(a, 1e-37)))))
    root = jnp.where(a < 1e-37, 0.0, root) * inverse
    return jnp.where(c < 0.0, -root, root)


def pack(value, scale):
    lanes = value.shape[1] // 2
    flat = jnp.concatenate([value[:, :lanes], value[:, lanes:]], axis=0)
    return encode(flat, scale), jnp.broadcast_to(scale, (SCALE_ROWS, lanes)).astype(bf16)


def unpack(code):
    rows = code.shape[0] - SCALE_ROWS
    inverse = 1.0 / code[rows : rows + 1, :].astype(f32)
    flat = decode(code[:rows, :], inverse)
    return jnp.concatenate([flat[: rows // 2], flat[rows // 2 :]], axis=1)


def kernel(
    img_ref, filt_ref, cot_ref, out_ref, ig_ref, fg_ref,
    F2, G, G2, cots, S, dF, codes, got, FIN, O, OR, IGB, IGR, IGX, IGS, IGZ,
    f_sem, a_send, a_recv, b_send, b_recv, p_send, p_recv, c_send, c_recv, h_send, h_recv,
    rs_send, rs_recv, o_send, o_recv, ig_send, ig_recv, fz_send, fz_recv, fy_send, fy_recv,
):
    f, r = lax.axis_index("filt"), lax.axis_index("rows")
    x, zh, core = f // (ZH * CORES), (f // CORES) % ZH, f % CORES
    y, q = r // ZL, r % ZL
    chans, width = img_ref.shape
    part = chans // ZL
    stack = TAPS * chans

    def dev(f_to, r_to):
        return {"filt": f_to, "rows": r_to}

    def x_peer(d):
        return dev(((x + d) % X) * (ZH * CORES) + zh * CORES + core, r)

    def zl_peer(d):
        return dev(f, y * ZL + (q + d) % ZL)

    def y_peer(d):
        return dev(f, ((y + d) % Y) * ZL + q)

    partner = f + CORES - 2 * CORES * zh
    sibling = f + 1 - 2 * core
    zh_dev, core_dev = dev(partner, r), dev(sibling, r)

    sends = []

    def zh_peer(d):
        return dev(partner, y * ZL + (q + d) % ZL)

    def send(src, dst, s_sem, r_sem, to):
        copy = pltpu.make_async_remote_copy(
            src_ref=src, dst_ref=dst, send_sem=s_sem, recv_sem=r_sem,
            device_id=to, device_id_type=pl.DeviceIdType.MESH,
        )
        copy.start()
        return copy

    def arrived(dst, r_sem):
        pltpu.make_async_remote_copy(
            src_ref=dst, dst_ref=dst, send_sem=r_sem, recv_sem=r_sem,
            device_id=core_dev, device_id_type=pl.DeviceIdType.MESH,
        ).wait_recv()

    def g_block(k):
        return G.at[pl.ds(pl.multiple_of(k * chans, chans), chans), :]

    load_img = pltpu.make_async_copy(img_ref, g_block(f), f_sem.at[0])
    load_cot = pltpu.make_async_copy(cot_ref, cots.at[q + 1], f_sem.at[1])
    load_f = pltpu.make_async_copy(filt_ref, F2, f_sem.at[2])
    for load in (load_img, load_cot, load_f):
        load.start()

    barrier = pltpu.get_barrier_semaphore()

    def greet(to):
        pl.semaphore_signal(barrier, inc=1, device_id=to, device_id_type=pl.DeviceIdType.MESH)

    fixed = [x_peer(d) for d in range(1, X)] + [zl_peer(d) for d in range(1, ZL)]
    fixed += [y_peer(d) for d in range(1, Y)] + [core_dev] + [zh_peer(d) for d in range(ZL)]
    for to in fixed:
        greet(to)

    below, above = (y > 0) & (q == 0), (y < Y - 1) & (q == ZL - 1)

    @pl.when(below)
    def _():
        greet(dev(f, r - 1))

    @pl.when(above)
    def _():
        greet(dev(f, r + 1))

    def g2_rows(k, to=q):
        at = 8 * (k // 8) + (to + 4 * (k % 2) + (k % 8) // 2) % 8
        return pl.ds(pl.multiple_of(at * part, part), part)

    def g2_block(k):
        return G2.at[g2_rows(k), :]

    def g2_piece(k, row, to=q):
        return G2.at[g2_rows(k, to), pl.ds(pl.multiple_of(row * width, width), width)]

    load_img.wait()
    load_cot.wait()
    g2_piece(f, q)[...] = G[pl.ds(pl.multiple_of(f * chans + q * part, part), part), :]
    others = jnp.where(below, 1, 0) + jnp.where(above, 1, 0)
    pl.semaphore_wait(barrier, len(fixed) + others)

    for d in list(range(ZL, 2 * ZL)) + list(range(1, ZL)):
        to = (q + d) % ZL
        sends.append(send(
            G.at[pl.ds(pl.multiple_of(f * chans + to * part, part), part), :], g2_piece(f, q, to),
            p_send.at[d], p_recv.at[d], zl_peer(d) if d < ZL else zh_peer(d),
        ))

    def gather_own(block, s_sem, r_sem):
        mine = block(f)
        for d in range(1, X):
            sends.append(send(mine, mine, s_sem.at[d], r_sem.at[d], x_peer(d)))
        sends.append(send(mine, mine, s_sem.at[4], r_sem.at[4], core_dev))

    def gather_other(block, s_sem, r_sem):
        other = block(partner)
        for d in range(1, X):
            sends.append(send(other, other, s_sem.at[4 + d], r_sem.at[4 + d], x_peer(d)))
        sends.append(send(other, other, s_sem.at[8], r_sem.at[8], core_dev))

    def gather_third(block, s_sem, r_sem):
        for d in range(1, X):
            x_from = ((x - d) % X) * (ZH * CORES) + core
            for second in range(2):
                k = x_from + CORES * (zh if second == 0 else 1 - zh)
                theirs = block(k)
                arrived(theirs, r_sem.at[d + 4 * second])
                at = 9 + 2 * (d - 1) + second
                sends.append(send(theirs, theirs, s_sem.at[at], r_sem.at[at], core_dev))

    def gather_last(block, s_sem, r_sem):
        base = 1 - core
        arrived(block(sibling), r_sem.at[4])
        arrived(block(partner + 1 - 2 * core), r_sem.at[8])
        for d in range(1, X):
            x_from = ((x - d) % X) * (ZH * CORES) + base
            for second in range(2):
                k = x_from + CORES * (zh if second == 0 else 1 - zh)
                arrived(block(k), r_sem.at[9 + 2 * (d - 1) + second])

    for d in range(1, ZL):
        mine = cots.at[q + 1]
        sends.append(send(mine, mine, c_send.at[d], c_recv.at[d], zl_peer(d)))

    gather_own(g_block, a_send, a_recv)

    def halo_copy(side):
        source, slot, step = (ZL, 0, 1) if side == 0 else (1, ZL + 1, -1)
        return pltpu.make_async_remote_copy(
            src_ref=cots.at[source], dst_ref=cots.at[slot], send_sem=h_send.at[side],
            recv_sem=h_recv.at[side], device_id=y_peer(step), device_id_type=pl.DeviceIdType.MESH,
        )

    def build(j):
        value = cots[j].astype(f32)
        for b in range(TAPS):
            at = j * width if isinstance(j, int) else pl.multiple_of(j * width, width)
            S[b * chans : (b + 1) * chans, pl.ds(at, width)] = shifted(value, b - 1).astype(bf16)

    build(q + 1)

    @pl.when(y == 0)
    def _():
        cots[0] = jnp.zeros((chans, width), bf16)

    @pl.when(y == Y - 1)
    def _():
        cots[ZL + 1] = jnp.zeros((chans, width), bf16)

    for d in range(1, ZL):
        arrived(g2_piece(f, (q - d) % ZL), p_recv.at[d])
    gather_own(g2_block, b_send, b_recv)
    sends.append(send(g_block(f), g_block(f), a_send.at[0], a_recv.at[0], zh_dev))
    for d in range(ZL):
        arrived(g2_piece(partner, (q - d) % ZL), p_recv.at[ZL + d])
    gather_other(g2_block, b_send, b_recv)

    for d in range(1, ZL):
        arrived(cots.at[(q - d) % ZL + 1], c_recv.at[d])

    @pl.when(y < Y - 1)
    def _():
        halo_copy(0).start()

    @pl.when(y > 0)
    def _():
        halo_copy(1).start()

    for d in range(1, ZL):
        build((q - d) % ZL + 1)

    gather_third(g2_block, b_send, b_recv)

    gather_last(g2_block, b_send, b_recv)

    arrived(g_block(partner), a_recv.at[0])
    gather_other(g_block, a_send, a_recv)

    def grad_term(a, first, last):
        at = (2 - a + first) * width
        return lax.dot_general(
            S[:, at : at + (last - first) * width], G2[:, first * width : last * width],
            (((1,), (1,)), ((), ())), preferred_element_type=f32,
        )

    dF[stack : 2 * stack, :] = grad_term(1, 0, ZL)
    dF[:stack, :] = grad_term(0, 0, ZL - 1)
    dF[2 * stack :, :] = grad_term(2, 1, ZL)

    @pl.when(y > 0)
    def _():
        arrived(cots.at[0], h_recv.at[0])

    @pl.when(y < Y - 1)
    def _():
        arrived(cots.at[ZL + 1], h_recv.at[1])

    build(0)
    build(ZL + 1)

    dF[:stack, :] += grad_term(0, ZL - 1, ZL)
    dF[2 * stack :, :] += grad_term(2, 0, 1)
    rows = TAPS * stack // Y
    scale = scale_for(dF[...])
    for k in range(Y):
        code, tail = pack(dF[rows * k : rows * (k + 1), :], scale)
        codes[k, : 2 * rows, :] = code
        codes[k, 2 * rows :, :] = tail
    for d in range(1, Y):
        sends.append(send(codes.at[(y + d) % Y], got.at[d], rs_send.at[d], rs_recv.at[d], y_peer(d)))

    load_f.wait()
    groups = X * ZH * CORES
    cols = width // groups
    half = width // 2
    for p in range(2):
        total = None
        for a in range(TAPS):
            at = pl.multiple_of((q + 2 - a) * width + p * half, half)
            term = lax.dot_general(
                S[:, pl.ds(at, half)], F2[a * stack : (a + 1) * stack, :],
                (((0,), (0,)), ((), ())), preferred_element_type=f32,
            )
            total = term if total is None else total + term
        for k in range(groups // 2):
            g = p * (groups // 2) + k
            IGB[g % CORES, g // (ZH * CORES), (g // CORES) % ZH] = total[cols * k : cols * (k + 1)]
    sends.append(send(IGB.at[1 - core], IGR, ig_send.at[0], ig_recv.at[0], core_dev))


    gather_third(g_block, a_send, a_recv)

    gather_last(g_block, a_send, a_recv)
    for a in (0, 2, 1):
        total = None
        taps = jnp.dot(F2[a * stack : (a + 1) * stack, :], G[...], preferred_element_type=f32)
        for b in range(TAPS):
            term = shifted(taps[b * chans : (b + 1) * chans], 1 - b)
            total = term if total is None else total + term
        O[a] = total

    def out_copy(a):
        return pltpu.make_async_remote_copy(
            src_ref=O.at[a], dst_ref=OR.at[a // 2], send_sem=o_send.at[a // 2], recv_sem=o_recv.at[a // 2],
            device_id=dev(f, r + 1 - a), device_id_type=pl.DeviceIdType.MESH,
        )

    arrived(IGR, ig_recv.at[0])
    for k in range(X):
        IGB[core, k] = IGB[core, k] + IGR[k]
    for d in range(1, X):
        sends.append(send(IGB.at[core, (x + d) % X], IGX.at[d], ig_send.at[d], ig_recv.at[d], x_peer(d)))


    piece = dF[pl.ds(pl.multiple_of(y * rows, rows), rows), :]
    for d in range(1, Y):
        arrived(got.at[d], rs_recv.at[d])
        piece = piece + unpack(got[d])
    piece = piece / jnp.sqrt(f32(Y * ZL * width))
    code, tail = pack(piece, scale_for(piece))
    FIN[y, q, : 2 * rows, :] = code
    FIN[y, q, 2 * rows :, :] = tail
    def quarter(c):
        return (q + c) % ZL

    def crosses(step, way, c):
        return step < Y // 2 or c % 2 == way

    def ring(step, way, c):
        at = (y - (step - 1)) % Y if way == 0 else (y + (step - 1)) % Y
        ref = FIN.at[at, quarter(c)]
        to = y_peer(1 if way == 0 else -1)
        sends.append(send(ref, ref, fy_send.at[way, step, c], fy_recv.at[way, step, c], to))

    def ring_arrived(step, way, c):
        at = (y - step) % Y if way == 0 else (y + step) % Y
        arrived(FIN.at[at, quarter(c)], fy_recv.at[way, step, c])

    def pass_on(step, c):
        for way in range(2):
            if crosses(step, way, c):
                ring_arrived(step, way, c)
                if step < Y // 2 and crosses(step + 1, way, c):
                    ring(step + 1, way, c)

    early = list(sends)
    sends.clear()
    for way in range(2):
        ring(1, way, 0)
    for d in range(1, ZL):
        sends.append(send(FIN.at[y, q], FIN.at[y, q], fz_send.at[d], fz_recv.at[d], zl_peer(d)))

    pass_on(1, 0)
    for c in range(1, ZL):
        arrived(FIN.at[y, quarter(c)], fz_recv.at[ZL - c])
        for way in range(2):
            ring(1, way, c)

    @pl.when(r < Y * ZL - 1)
    def _():
        out_copy(0).start()

    @pl.when(r > 0)
    def _():
        out_copy(2).start()

    lane_group = lax.broadcasted_iota(jnp.int32, (rows, 128), 1) // 16

    def result(at):
        quarters = [unpack(FIN[at, k]) for k in range(ZL)]
        for t in range(8):
            half_at, j = t // 4, t % 4
            mine = (lane_group + (8 - j)) % ZL
            tile = quarters[0][:, 128 * half_at : 128 * (half_at + 1)]
            for k in range(1, ZL):
                tile = jnp.where(mine == k, quarters[k][:, 128 * half_at : 128 * (half_at + 1)], tile)
            if j:
                tile = pltpu.roll(tile, 128 - 16 * j, 1)
            fg_ref[pl.ds(pl.multiple_of(at * rows, 8), rows), 128 * t : 128 * (t + 1)] = tile

    result(y)
    for step in range(1, Y // 2 + 1):
        for c in range(1, ZL):
            pass_on(step, c)
        if step < Y // 2:
            pass_on(step + 1, 0)
            result((y - step) % Y)
            result((y + step) % Y)
        if step == 1:
            IGS[...] = IGB[core, x]
            for d in range(1, X):
                arrived(IGX.at[d], ig_recv.at[d])
                IGS[...] = IGS[...] + IGX[d]
            sends.append(send(IGS.at[1 - zh], IGZ, ig_send.at[X], ig_recv.at[X], zh_dev))
            for copy in early:
                copy.wait_send()
    result((y + Y // 2) % Y)

    OUT = O.at[1]

    @pl.when(r > 0)
    def _():
        arrived(OR.at[0], o_recv.at[0])
        OUT[...] = OUT[...] + OR[0]

    @pl.when(r < Y * ZL - 1)
    def _():
        arrived(OR.at[1], o_recv.at[1])
        OUT[...] = OUT[...] + OR[1]

    out_ref[...] = OUT[...].astype(bf16)
    arrived(IGZ, ig_recv.at[X])
    ig_ref[...] = (IGS[zh] + IGZ[...]).astype(bf16)

    for copy in sends:
        copy.wait_send()

    @pl.when(y < Y - 1)
    def _():
        halo_copy(0).wait_send()

    @pl.when(y > 0)
    def _():
        halo_copy(1).wait_send()

    @pl.when(r < Y * ZL - 1)
    def _():
        out_copy(0).wait_send()

    @pl.when(r > 0)
    def _():
        out_copy(2).wait_send()


def on_device(images, filters, cotangent):
    _, chans, width = images.shape
    taps, total = filters.shape[1:]
    groups = X * ZH * CORES
    cols = width // groups
    stack = TAPS * chans
    piece = taps * chans // Y
    quarter = total // ZL
    dma = pltpu.SemaphoreType.DMA
    operands = images[0], jnp.transpose(filters, (1, 0, 2)).reshape(stack * TAPS, total), cotangent[0]
    vmem = pltpu.VMEM
    hbm_spec = pl.BlockSpec(memory_space=pltpu.HBM)
    vmem_spec = pl.BlockSpec(memory_space=pltpu.VMEM)
    code = (2 * piece + SCALE_ROWS, quarter // 2)
    output, input_grad, grad = pl.pallas_call(
        kernel,
        out_shape=(
            jax.ShapeDtypeStruct((chans, width), bf16),
            jax.ShapeDtypeStruct((cols, total), bf16),
            jax.ShapeDtypeStruct((taps * chans, total), f32),
        ),
        in_specs=[hbm_spec] * 3,
        out_specs=(vmem_spec, vmem_spec, vmem_spec),
        scratch_shapes=[
            vmem((taps * chans, total), bf16),
            vmem((total, width), bf16),
            vmem((quarter, ZL * width), bf16),
            vmem((ZL + 2, chans, width), bf16),
            vmem((stack, (ZL + 2) * width), bf16),
            vmem((taps * chans, quarter), f32),
            vmem((Y,) + code, bf16),
            vmem((Y,) + code, bf16),
            vmem((Y, ZL) + code, bf16),
            vmem((TAPS, chans, width), f32),
            vmem((2, chans, width), f32),
            vmem((CORES, X, ZH, cols, total), f32),
            vmem((X, ZH, cols, total), f32),
            vmem((X, ZH, cols, total), f32),
            vmem((ZH, cols, total), f32),
            vmem((cols, total), f32),
            dma((3,)),
            dma((15,)), dma((15,)),
            dma((15,)), dma((15,)),
            dma((2 * ZL,)), dma((2 * ZL,)),
            dma((ZL,)), dma((ZL,)),
            dma((2,)), dma((2,)),
            dma((Y,)), dma((Y,)),
            dma((2,)), dma((2,)),
            dma((X + 1,)), dma((X + 1,)),
            dma((ZL,)), dma((ZL,)),
            dma((2, Y, ZL)), dma((2, Y, ZL)),
        ],
        compiler_params=pltpu.CompilerParams(
            collective_id=0, has_side_effects=True, vmem_limit_bytes=48 * 1024 * 1024
        ),
    )(*(pltpu.with_memory_space_constraint(a, pltpu.HBM) for a in operands))
    grad = jnp.transpose(grad.reshape(taps, chans, total), (1, 0, 2))
    return output[None], input_grad[None], grad


def solution(mesh):
    return jax.shard_map(
        on_device,
        mesh=mesh,
        in_specs=(P("rows", "filt", None), P("filt", None, None), P("rows", "filt", None)),
        out_specs=(P("rows", "filt", None), P("rows", "filt", None), P("filt", None, None)),
        check_vma=False,
    )
```

```python
import functools

import jax
import jax.numpy as jnp
from jax import lax
from jax.experimental import pallas as pl
from jax.experimental.pallas import tpu as pltpu
from jax.sharding import PartitionSpec as P

X, ZH, CORES = 4, 2, 2
Y, ZL = 8, 4
TAPS = 3
SCALE_ROWS = 16
TOP = 200.0
f32 = jnp.float32
bf16 = jnp.bfloat16


def shifted(value, by):
    if by == 0:
        return value
    width = value.shape[1]
    column = lax.broadcasted_iota(jnp.int32, value.shape, 1)
    rolled = pltpu.roll(value, by % width, 1)
    return jnp.where(column == (0 if by == 1 else width - 1), 0.0, rolled)


def scale_for(block):
    largest = jnp.max(jnp.abs(block), axis=(0, 1), keepdims=True)
    return (TOP / jnp.maximum(largest, 1e-30)).astype(bf16).astype(f32)


def encode(value, scale):
    t = value * scale
    t2 = t * t
    t4 = t2 * t2
    t8 = t4 * t4
    t16 = t8 * t8
    return jnp.where(t < 0.0, -t16, t16).astype(bf16)


def decode(code, inverse):
    c = code.astype(f32)
    a = jnp.abs(c)
    root = lax.rsqrt(lax.rsqrt(lax.rsqrt(lax.rsqrt(jnp.maximum(a, 1e-37)))))
    root = jnp.where(a < 1e-37, 0.0, root) * inverse
    return jnp.where(c < 0.0, -root, root)


def coded(value):
    scale = scale_for(value)
    return encode(value, scale), jnp.broadcast_to(scale, (SCALE_ROWS, value.shape[1])).astype(bf16)


def decoded(code):
    rows = code.shape[0] - SCALE_ROWS
    return decode(code[:rows, :], 1.0 / code[rows : rows + 1, :].astype(f32))


def pack(value, scale):
    lanes = value.shape[1] // 2
    flat = jnp.concatenate([value[:, :lanes], value[:, lanes:]], axis=0)
    return encode(flat, scale), jnp.broadcast_to(scale, (SCALE_ROWS, lanes)).astype(bf16)


def unpack(code):
    rows = code.shape[0] - SCALE_ROWS
    inverse = 1.0 / code[rows : rows + 1, :].astype(f32)
    flat = decode(code[:rows, :], inverse)
    return jnp.concatenate([flat[: rows // 2], flat[rows // 2 :]], axis=1)


def kernel(
    img_ref, filt_ref, cot_ref, out_ref, ig_ref, fg_ref,
    F2, G, G2, cots, S, dF, codes, got, FIN, O, OC, OR, IGB, IGR, IXC, IXR, IGS, IZC, IZR,
    f_sem, a_send, a_recv, b_send, b_recv, p_send, p_recv, c_send, c_recv, h_send, h_recv,
    rs_send, rs_recv, o_send, o_recv, ig_send, ig_recv, fz_send, fz_recv, fy_send, fy_recv,
    fo_send, fo_recv, fa_send, fa_recv,
):
    f, r = lax.axis_index("filt"), lax.axis_index("rows")
    x, zh, core = f // (ZH * CORES), (f // CORES) % ZH, f % CORES
    y, q = r // ZL, r % ZL
    chans, width = img_ref.shape
    part = chans // ZL
    stack = TAPS * chans

    def dev(f_to, r_to):
        return {"filt": f_to, "rows": r_to}

    def x_peer(d):
        return dev(((x + d) % X) * (ZH * CORES) + zh * CORES + core, r)

    def zl_peer(d):
        return dev(f, y * ZL + (q + d) % ZL)

    def y_peer(d):
        return dev(f, ((y + d) % Y) * ZL + q)

    partner = f + CORES - 2 * CORES * zh
    sibling = f + 1 - 2 * core
    zh_dev, core_dev = dev(partner, r), dev(sibling, r)

    sends = []

    def zh_peer(d):
        return dev(partner, y * ZL + (q + d) % ZL)

    def send(src, dst, s_sem, r_sem, to):
        copy = pltpu.make_async_remote_copy(
            src_ref=src, dst_ref=dst, send_sem=s_sem, recv_sem=r_sem,
            device_id=to, device_id_type=pl.DeviceIdType.MESH,
        )
        copy.start()
        return copy

    def arrived(dst, r_sem):
        pltpu.make_async_remote_copy(
            src_ref=dst, dst_ref=dst, send_sem=r_sem, recv_sem=r_sem,
            device_id=core_dev, device_id_type=pl.DeviceIdType.MESH,
        ).wait_recv()

    def g_block(k):
        return G.at[pl.ds(pl.multiple_of(k * chans, chans), chans), :]

    load_img = pltpu.make_async_copy(img_ref, g_block(f), f_sem.at[0])
    load_cot = pltpu.make_async_copy(cot_ref, cots.at[q + 1], f_sem.at[1])
    load_f = pltpu.make_async_copy(filt_ref, F2, f_sem.at[2])
    for load in (load_img, load_cot, load_f):
        load.start()

    barrier = pltpu.get_barrier_semaphore()

    def greet(to):
        pl.semaphore_signal(barrier, inc=1, device_id=to, device_id_type=pl.DeviceIdType.MESH)

    fixed = [x_peer(d) for d in range(1, X)] + [zl_peer(d) for d in range(1, ZL)]
    fixed += [y_peer(d) for d in range(1, Y)] + [core_dev] + [zh_peer(d) for d in range(ZL)]
    for to in fixed:
        greet(to)

    below, above = (y > 0) & (q == 0), (y < Y - 1) & (q == ZL - 1)

    @pl.when(below)
    def _():
        greet(dev(f, r - 1))

    @pl.when(above)
    def _():
        greet(dev(f, r + 1))

    def g2_rows(k, to=q):
        at = 8 * (k // 8) + (to + 4 * (k % 2) + (k % 8) // 2) % 8
        return pl.ds(pl.multiple_of(at * part, part), part)

    def g2_block(k):
        return G2.at[g2_rows(k), :]

    def g2_piece(k, row, to=q):
        return G2.at[g2_rows(k, to), pl.ds(pl.multiple_of(row * width, width), width)]

    load_img.wait()
    load_cot.wait()
    g2_piece(f, q)[...] = G[pl.ds(pl.multiple_of(f * chans + q * part, part), part), :]
    others = jnp.where(below, 1, 0) + jnp.where(above, 1, 0)
    pl.semaphore_wait(barrier, len(fixed) + others)

    for d in list(range(ZL, 2 * ZL)) + list(range(1, ZL)):
        to = (q + d) % ZL
        sends.append(send(
            G.at[pl.ds(pl.multiple_of(f * chans + to * part, part), part), :], g2_piece(f, q, to),
            p_send.at[d], p_recv.at[d], zl_peer(d) if d < ZL else zh_peer(d),
        ))

    def gather_own(block, s_sem, r_sem):
        mine = block(f)
        for d in range(1, X):
            sends.append(send(mine, mine, s_sem.at[d], r_sem.at[d], x_peer(d)))
        sends.append(send(mine, mine, s_sem.at[4], r_sem.at[4], core_dev))

    def gather_other(block, s_sem, r_sem):
        other = block(partner)
        for d in range(1, X):
            sends.append(send(other, other, s_sem.at[4 + d], r_sem.at[4 + d], x_peer(d)))
        sends.append(send(other, other, s_sem.at[8], r_sem.at[8], core_dev))

    def gather_third(block, s_sem, r_sem, second):
        for d in range(1, X):
            k = ((x - d) % X) * (ZH * CORES) + core + CORES * (zh if second == 0 else 1 - zh)
            theirs = block(k)
            arrived(theirs, r_sem.at[d + 4 * second])
            at = 9 + 2 * (d - 1) + second
            sends.append(send(theirs, theirs, s_sem.at[at], r_sem.at[at], core_dev))

    def gather_last(block, s_sem, r_sem):
        base = 1 - core
        arrived(block(sibling), r_sem.at[4])
        arrived(block(partner + 1 - 2 * core), r_sem.at[8])
        for d in range(1, X):
            x_from = ((x - d) % X) * (ZH * CORES) + base
            for second in range(2):
                k = x_from + CORES * (zh if second == 0 else 1 - zh)
                arrived(block(k), r_sem.at[9 + 2 * (d - 1) + second])

    for d in range(1, ZL):
        mine = cots.at[q + 1]
        sends.append(send(mine, mine, c_send.at[d], c_recv.at[d], zl_peer(d)))

    gather_own(g_block, a_send, a_recv)

    def halo_copy(side):
        source, slot, step = (ZL, 0, 1) if side == 0 else (1, ZL + 1, -1)
        return pltpu.make_async_remote_copy(
            src_ref=cots.at[source], dst_ref=cots.at[slot], send_sem=h_send.at[side],
            recv_sem=h_recv.at[side], device_id=y_peer(step), device_id_type=pl.DeviceIdType.MESH,
        )

    def build(j):
        value = cots[j].astype(f32)
        for b in range(TAPS):
            at = j * width if isinstance(j, int) else pl.multiple_of(j * width, width)
            S[b * chans : (b + 1) * chans, pl.ds(at, width)] = shifted(value, b - 1).astype(bf16)

    build(q + 1)

    @pl.when(y == 0)
    def _():
        cots[0] = jnp.zeros((chans, width), bf16)

    @pl.when(y == Y - 1)
    def _():
        cots[ZL + 1] = jnp.zeros((chans, width), bf16)

    for d in range(1, ZL):
        arrived(g2_piece(f, (q - d) % ZL), p_recv.at[d])
    gather_own(g2_block, b_send, b_recv)
    sends.append(send(g_block(f), g_block(f), a_send.at[0], a_recv.at[0], zh_dev))
    for d in range(ZL):
        arrived(g2_piece(partner, (q - d) % ZL), p_recv.at[ZL + d])
    gather_other(g2_block, b_send, b_recv)

    gather_third(g2_block, b_send, b_recv, 0)
    for d in range(1, ZL):
        arrived(cots.at[(q - d) % ZL + 1], c_recv.at[d])

    @pl.when(y < Y - 1)
    def _():
        halo_copy(0).start()

    @pl.when(y > 0)
    def _():
        halo_copy(1).start()

    for d in range(1, ZL):
        build((q - d) % ZL + 1)

    gather_third(g2_block, b_send, b_recv, 1)

    gather_last(g2_block, b_send, b_recv)

    arrived(g_block(partner), a_recv.at[0])
    gather_other(g_block, a_send, a_recv)

    def grad_term(a, first, last):
        at = (2 - a + first) * width
        return lax.dot_general(
            S[:, at : at + (last - first) * width], G2[:, first * width : last * width],
            (((1,), (1,)), ((), ())), preferred_element_type=f32,
        )

    dF[stack : 2 * stack, :] = grad_term(1, 0, ZL)
    dF[:stack, :] = grad_term(0, 0, ZL - 1)
    dF[2 * stack :, :] = grad_term(2, 1, ZL)

    @pl.when(y > 0)
    def _():
        arrived(cots.at[0], h_recv.at[0])

    @pl.when(y < Y - 1)
    def _():
        arrived(cots.at[ZL + 1], h_recv.at[1])

    build(0)
    build(ZL + 1)

    dF[:stack, :] += grad_term(0, ZL - 1, ZL)
    dF[2 * stack :, :] += grad_term(2, 0, 1)
    rows = TAPS * stack // Y
    scale = scale_for(dF[...])
    for k in range(Y):
        code, tail = pack(dF[rows * k : rows * (k + 1), :], scale)
        codes[k, : 2 * rows, :] = code
        codes[k, 2 * rows :, :] = tail
    for d in range(1, Y):
        sends.append(send(codes.at[(y + d) % Y], got.at[d], rs_send.at[d], rs_recv.at[d], y_peer(d)))

    load_f.wait()
    groups = X * ZH * CORES
    cols = width // groups
    half = width // 2
    for p in range(2):
        total = None
        for a in range(TAPS):
            at = pl.multiple_of((q + 2 - a) * width + p * half, half)
            term = lax.dot_general(
                S[:, pl.ds(at, half)], F2[a * stack : (a + 1) * stack, :],
                (((0,), (0,)), ((), ())), preferred_element_type=f32,
            )
            total = term if total is None else total + term
        for k in range(groups // 2):
            g = p * (groups // 2) + k
            IGB[g % CORES, g // (ZH * CORES), (g // CORES) % ZH] = total[cols * k : cols * (k + 1)]
    sends.append(send(IGB.at[1 - core], IGR, ig_send.at[0], ig_recv.at[0], core_dev))


    gather_third(g_block, a_send, a_recv, 0)
    gather_third(g_block, a_send, a_recv, 1)

    arrived(IGR, ig_recv.at[0])
    deep = ZH * cols
    for d in range(1, X):
        to = (x + d) % X
        code, tail = coded((IGB[core, to] + IGR[to]).reshape(deep, -1))
        IXC[d, :deep, :] = code
        IXC[d, deep:, :] = tail
        sends.append(send(IXC.at[d], IXR.at[d], ig_send.at[d], ig_recv.at[d], x_peer(d)))
    IGS[...] = IGB[core, x] + IGR[x]

    gather_last(g_block, a_send, a_recv)
    for a in (0, 2, 1):
        total = None
        taps = jnp.dot(F2[a * stack : (a + 1) * stack, :], G[...], preferred_element_type=f32)
        for b in range(TAPS):
            term = shifted(taps[b * chans : (b + 1) * chans], 1 - b)
            total = term if total is None else total + term
        if a == 1:
            O[...] = total
        else:
            code, tail = coded(total)
            OC[a // 2, :chans, :] = code
            OC[a // 2, chans:, :] = tail

    def out_copy(a):
        return pltpu.make_async_remote_copy(
            src_ref=OC.at[a // 2], dst_ref=OR.at[a // 2], send_sem=o_send.at[a // 2], recv_sem=o_recv.at[a // 2],
            device_id=dev(f, r + 1 - a), device_id_type=pl.DeviceIdType.MESH,
        )

    piece = dF[pl.ds(pl.multiple_of(y * rows, rows), rows), :]
    for d in range(1, Y):
        arrived(got.at[d], rs_recv.at[d])
        piece = piece + unpack(got[d])
    piece = piece / jnp.sqrt(f32(Y * ZL * width))
    code, tail = pack(piece, scale_for(piece))
    FIN[y, q, : 2 * rows, :] = code
    FIN[y, q, 2 * rows :, :] = tail
    opposite = Y // 2

    def quarter(c):
        return (q + c) % ZL

    def ring(step, way, c):
        at = (y - (step - 1)) % Y if way == 0 else (y + (step - 1)) % Y
        ref = FIN.at[at, quarter(c)]
        to = y_peer(1 if way == 0 else -1)
        sends.append(send(ref, ref, fy_send.at[way, step, c], fy_recv.at[way, step, c], to))

    def ring_arrived(step, way, c):
        at = (y - step) % Y if way == 0 else (y + step) % Y
        arrived(FIN.at[at, quarter(c)], fy_recv.at[way, step, c])

    def pass_on(step, c):
        for way in range(2):
            ring_arrived(step, way, c)
            if step + 1 < opposite:
                ring(step + 1, way, c)

    def over_z(at, s_sem, r_sem):
        mine = FIN.at[at, q]
        for d in range(1, ZL):
            sends.append(send(mine, mine, s_sem.at[d], r_sem.at[d], zl_peer(d)))

    early = list(sends)
    sends.clear()
    sends.append(send(FIN.at[y, q], FIN.at[y, q], fo_send, fo_recv, y_peer(opposite)))
    over_z(y, fz_send, fz_recv)
    for way in range(2):
        ring(1, way, 0)

    pass_on(1, 0)
    for c in range(1, ZL):
        arrived(FIN.at[y, quarter(c)], fz_recv.at[ZL - c])
        for way in range(2):
            ring(1, way, c)
    across = (y + opposite) % Y
    arrived(FIN.at[across, q], fo_recv)
    over_z(across, fa_send, fa_recv)

    @pl.when(r < Y * ZL - 1)
    def _():
        out_copy(0).start()

    @pl.when(r > 0)
    def _():
        out_copy(2).start()

    lane_group = lax.broadcasted_iota(jnp.int32, (rows, 128), 1) // 16

    def result(at):
        quarters = [unpack(FIN[at, k]) for k in range(ZL)]
        for t in range(8):
            half_at, j = t // 4, t % 4
            mine = (lane_group + (8 - j)) % ZL
            tile = quarters[0][:, 128 * half_at : 128 * (half_at + 1)]
            for k in range(1, ZL):
                tile = jnp.where(mine == k, quarters[k][:, 128 * half_at : 128 * (half_at + 1)], tile)
            if j:
                tile = pltpu.roll(tile, 128 - 16 * j, 1)
            fg_ref[pl.ds(pl.multiple_of(at * rows, 8), rows), 128 * t : 128 * (t + 1)] = tile

    result(y)
    for d in range(1, X):
        arrived(IXR.at[d], ig_recv.at[d])
        IGS[...] = IGS[...] + decoded(IXR[d]).reshape(IGS.shape)
    code, tail = coded(IGS[1 - zh])
    IZC[:cols, :] = code
    IZC[cols:, :] = tail
    sends.append(send(IZC, IZR, ig_send.at[X], ig_recv.at[X], zh_dev))
    for copy in early:
        copy.wait_send()

    for step in range(1, opposite):
        for c in range(1, ZL):
            pass_on(step, c)
        if step + 1 < opposite:
            pass_on(step + 1, 0)
        result((y - step) % Y)
        result((y + step) % Y)
    for c in range(1, ZL):
        arrived(FIN.at[across, quarter(c)], fa_recv.at[ZL - c])
    result(across)

    @pl.when(r > 0)
    def _():
        arrived(OR.at[0], o_recv.at[0])
        O[...] = O[...] + decoded(OR[0])

    @pl.when(r < Y * ZL - 1)
    def _():
        arrived(OR.at[1], o_recv.at[1])
        O[...] = O[...] + decoded(OR[1])

    out_ref[...] = O[...].astype(bf16)
    arrived(IZR, ig_recv.at[X])
    ig_ref[...] = (IGS[zh] + decoded(IZR[...])).astype(bf16)

    for copy in sends:
        copy.wait_send()

    @pl.when(y < Y - 1)
    def _():
        halo_copy(0).wait_send()

    @pl.when(y > 0)
    def _():
        halo_copy(1).wait_send()

    @pl.when(r < Y * ZL - 1)
    def _():
        out_copy(0).wait_send()

    @pl.when(r > 0)
    def _():
        out_copy(2).wait_send()


def on_device(images, filters, cotangent):
    _, chans, width = images.shape
    taps, total = filters.shape[1:]
    groups = X * ZH * CORES
    cols = width // groups
    stack = TAPS * chans
    piece = taps * chans // Y
    quarter = total // ZL
    dma = pltpu.SemaphoreType.DMA
    operands = images[0], jnp.transpose(filters, (1, 0, 2)).reshape(stack * TAPS, total), cotangent[0]
    vmem = pltpu.VMEM
    hbm_spec = pl.BlockSpec(memory_space=pltpu.HBM)
    vmem_spec = pl.BlockSpec(memory_space=pltpu.VMEM)
    code = (2 * piece + SCALE_ROWS, quarter // 2)
    output, input_grad, grad = pl.pallas_call(
        kernel,
        out_shape=(
            jax.ShapeDtypeStruct((chans, width), bf16),
            jax.ShapeDtypeStruct((cols, total), bf16),
            jax.ShapeDtypeStruct((taps * chans, total), f32),
        ),
        in_specs=[hbm_spec] * 3,
        out_specs=(vmem_spec, vmem_spec, vmem_spec),
        scratch_shapes=[
            vmem((taps * chans, total), bf16),
            vmem((total, width), bf16),
            vmem((quarter, ZL * width), bf16),
            vmem((ZL + 2, chans, width), bf16),
            vmem((stack, (ZL + 2) * width), bf16),
            vmem((taps * chans, quarter), f32),
            vmem((Y,) + code, bf16),
            vmem((Y,) + code, bf16),
            vmem((Y, ZL) + code, bf16),
            vmem((chans, width), f32),
            vmem((2, chans + SCALE_ROWS, width), bf16),
            vmem((2, chans + SCALE_ROWS, width), bf16),
            vmem((CORES, X, ZH, cols, total), f32),
            vmem((X, ZH, cols, total), f32),
            vmem((X, ZH * cols + SCALE_ROWS, total), bf16),
            vmem((X, ZH * cols + SCALE_ROWS, total), bf16),
            vmem((ZH, cols, total), f32),
            vmem((cols + SCALE_ROWS, total), bf16),
            vmem((cols + SCALE_ROWS, total), bf16),
            dma((3,)),
            dma((15,)), dma((15,)),
            dma((15,)), dma((15,)),
            dma((2 * ZL,)), dma((2 * ZL,)),
            dma((ZL,)), dma((ZL,)),
            dma((2,)), dma((2,)),
            dma((Y,)), dma((Y,)),
            dma((2,)), dma((2,)),
            dma((X + 1,)), dma((X + 1,)),
            dma((ZL,)), dma((ZL,)),
            dma((2, Y // 2, ZL)), dma((2, Y // 2, ZL)),
            dma, dma,
            dma((ZL,)), dma((ZL,)),
        ],
        compiler_params=pltpu.CompilerParams(
            collective_id=0, has_side_effects=True, vmem_limit_bytes=48 * 1024 * 1024
        ),
    )(*(pltpu.with_memory_space_constraint(a, pltpu.HBM) for a in operands))
    grad = jnp.transpose(grad.reshape(taps, chans, total), (1, 0, 2))
    return output[None], input_grad[None], grad


def solution(mesh):
    return jax.shard_map(
        on_device,
        mesh=mesh,
        in_specs=(P("rows", "filt", None), P("filt", None, None), P("rows", "filt", None)),
        out_specs=(P("rows", "filt", None), P("rows", "filt", None), P("filt", None, None)),
        check_vma=False,
    )
```

```python
import functools

import jax
import jax.numpy as jnp
from jax import lax
from jax.experimental import pallas as pl
from jax.experimental.pallas import tpu as pltpu
from jax.sharding import PartitionSpec as P

X, ZH, CORES = 4, 2, 2
Y, ZL = 8, 4
TAPS = 3
SCALE_ROWS = 16
TOP = 200.0
f32 = jnp.float32
bf16 = jnp.bfloat16


def shifted(value, by):
    if by == 0:
        return value
    width = value.shape[1]
    column = lax.broadcasted_iota(jnp.int32, value.shape, 1)
    rolled = pltpu.roll(value, by % width, 1)
    return jnp.where(column == (0 if by == 1 else width - 1), 0.0, rolled)


def scale_for(block):
    largest = jnp.max(jnp.abs(block), axis=(0, 1), keepdims=True)
    return (TOP / jnp.maximum(largest, 1e-30)).astype(bf16).astype(f32)


def encode(value, scale):
    t = value * scale
    t2 = t * t
    t4 = t2 * t2
    t8 = t4 * t4
    t16 = t8 * t8
    return jnp.where(t < 0.0, -t16, t16).astype(bf16)


def decode(code, inverse):
    c = code.astype(f32)
    a = jnp.abs(c)
    root = lax.rsqrt(lax.rsqrt(lax.rsqrt(lax.rsqrt(jnp.maximum(a, 1e-37)))))
    root = jnp.where(a < 1e-37, 0.0, root) * inverse
    return jnp.where(c < 0.0, -root, root)


def coded(value):
    scale = scale_for(value)
    return encode(value, scale), jnp.broadcast_to(scale, (SCALE_ROWS, value.shape[1])).astype(bf16)


def decoded(code):
    rows = code.shape[0] - SCALE_ROWS
    return decode(code[:rows, :], 1.0 / code[rows : rows + 1, :].astype(f32))


def pack(value, scale):
    lanes = value.shape[1] // 2
    flat = jnp.concatenate([value[:, :lanes], value[:, lanes:]], axis=0)
    return encode(flat, scale), jnp.broadcast_to(scale, (SCALE_ROWS, lanes)).astype(bf16)


def unpack(code):
    rows = code.shape[0] - SCALE_ROWS
    inverse = 1.0 / code[rows : rows + 1, :].astype(f32)
    flat = decode(code[:rows, :], inverse)
    return jnp.concatenate([flat[: rows // 2], flat[rows // 2 :]], axis=1)


def kernel(
    img_ref, filt_ref, cot_ref, out_ref, ig_ref, fg_ref,
    F2, G, G2, cots, S, dF, codes, got, FIN, O, OC, OR, IGB, IGR, IXC, IXR, IGS, IZC, IZR,
    f_sem, a_send, a_recv, b_send, b_recv, p_send, p_recv, c_send, c_recv, h_send, h_recv,
    rs_send, rs_recv, o_send, o_recv, ig_send, ig_recv, fz_send, fz_recv, fy_send, fy_recv,
    fo_send, fo_recv, fa_send, fa_recv,
):
    f, r = lax.axis_index("filt"), lax.axis_index("rows")
    x, zh, core = f // (ZH * CORES), (f // CORES) % ZH, f % CORES
    y, q = r // ZL, r % ZL
    chans, width = img_ref.shape
    part = chans // ZL
    stack = TAPS * chans

    def dev(f_to, r_to):
        return {"filt": f_to, "rows": r_to}

    def x_peer(d):
        return dev(((x + d) % X) * (ZH * CORES) + zh * CORES + core, r)

    def zl_peer(d):
        return dev(f, y * ZL + (q + d) % ZL)

    def y_peer(d):
        return dev(f, ((y + d) % Y) * ZL + q)

    partner = f + CORES - 2 * CORES * zh
    sibling = f + 1 - 2 * core
    zh_dev, core_dev = dev(partner, r), dev(sibling, r)

    sends = []

    def zh_peer(d):
        return dev(partner, y * ZL + (q + d) % ZL)

    def send(src, dst, s_sem, r_sem, to):
        copy = pltpu.make_async_remote_copy(
            src_ref=src, dst_ref=dst, send_sem=s_sem, recv_sem=r_sem,
            device_id=to, device_id_type=pl.DeviceIdType.MESH,
        )
        copy.start()
        return copy

    def arrived(dst, r_sem):
        pltpu.make_async_remote_copy(
            src_ref=dst, dst_ref=dst, send_sem=r_sem, recv_sem=r_sem,
            device_id=core_dev, device_id_type=pl.DeviceIdType.MESH,
        ).wait_recv()

    def g_block(k):
        return G.at[pl.ds(pl.multiple_of(k * chans, chans), chans), :]

    load_img = pltpu.make_async_copy(img_ref, g_block(f), f_sem.at[0])
    load_cot = pltpu.make_async_copy(cot_ref, cots.at[q + 1], f_sem.at[1])
    load_f = pltpu.make_async_copy(filt_ref, F2, f_sem.at[2])
    for load in (load_img, load_cot, load_f):
        load.start()

    barrier = pltpu.get_barrier_semaphore()

    def greet(to):
        pl.semaphore_signal(barrier, inc=1, device_id=to, device_id_type=pl.DeviceIdType.MESH)

    fixed = [x_peer(d) for d in range(1, X)] + [zl_peer(d) for d in range(1, ZL)]
    fixed += [y_peer(d) for d in range(1, Y)] + [core_dev] + [zh_peer(d) for d in range(ZL)]
    for to in fixed:
        greet(to)

    below, above = (y > 0) & (q == 0), (y < Y - 1) & (q == ZL - 1)

    @pl.when(below)
    def _():
        greet(dev(f, r - 1))

    @pl.when(above)
    def _():
        greet(dev(f, r + 1))

    def g2_rows(k, to=q):
        at = 8 * (k // 8) + (to + 4 * (k % 2) + (k % 8) // 2) % 8
        return pl.ds(pl.multiple_of(at * part, part), part)

    def g2_block(k):
        return G2.at[g2_rows(k), :]

    def g2_piece(k, row, to=q):
        return G2.at[g2_rows(k, to), pl.ds(pl.multiple_of(row * width, width), width)]

    load_img.wait()
    load_cot.wait()
    g2_piece(f, q)[...] = G[pl.ds(pl.multiple_of(f * chans + q * part, part), part), :]
    others = jnp.where(below, 1, 0) + jnp.where(above, 1, 0)
    pl.semaphore_wait(barrier, len(fixed) + others)

    for d in list(range(1, ZL)) + list(range(ZL, 2 * ZL)):
        to = (q + d) % ZL
        sends.append(send(
            G.at[pl.ds(pl.multiple_of(f * chans + to * part, part), part), :], g2_piece(f, q, to),
            p_send.at[d], p_recv.at[d], zl_peer(d) if d < ZL else zh_peer(d),
        ))

    def gather_own(block, s_sem, r_sem):
        mine = block(f)
        for d in (2, 1, 3):
            sends.append(send(mine, mine, s_sem.at[d], r_sem.at[d], x_peer(d)))
        sends.append(send(mine, mine, s_sem.at[4], r_sem.at[4], core_dev))

    def gather_other(block, s_sem, r_sem):
        other = block(partner)
        for d in (2, 1, 3):
            sends.append(send(other, other, s_sem.at[4 + d], r_sem.at[4 + d], x_peer(d)))
        sends.append(send(other, other, s_sem.at[8], r_sem.at[8], core_dev))

    def gather_third(block, s_sem, r_sem, second):
        for d in range(1, X):
            k = ((x - d) % X) * (ZH * CORES) + core + CORES * (zh if second == 0 else 1 - zh)
            theirs = block(k)
            arrived(theirs, r_sem.at[d + 4 * second])
            at = 9 + 2 * (d - 1) + second
            sends.append(send(theirs, theirs, s_sem.at[at], r_sem.at[at], core_dev))

    def gather_last(block, s_sem, r_sem):
        base = 1 - core
        arrived(block(sibling), r_sem.at[4])
        arrived(block(partner + 1 - 2 * core), r_sem.at[8])
        for d in range(1, X):
            x_from = ((x - d) % X) * (ZH * CORES) + base
            for second in range(2):
                k = x_from + CORES * (zh if second == 0 else 1 - zh)
                arrived(block(k), r_sem.at[9 + 2 * (d - 1) + second])

    for d in range(1, ZL):
        mine = cots.at[q + 1]
        sends.append(send(mine, mine, c_send.at[d], c_recv.at[d], zl_peer(d)))

    gather_own(g_block, a_send, a_recv)

    def halo_copy(side):
        source, slot, step = (ZL, 0, 1) if side == 0 else (1, ZL + 1, -1)
        return pltpu.make_async_remote_copy(
            src_ref=cots.at[source], dst_ref=cots.at[slot], send_sem=h_send.at[side],
            recv_sem=h_recv.at[side], device_id=y_peer(step), device_id_type=pl.DeviceIdType.MESH,
        )

    def build(j):
        value = cots[j].astype(f32)
        for b in range(TAPS):
            at = j * width if isinstance(j, int) else pl.multiple_of(j * width, width)
            S[b * chans : (b + 1) * chans, pl.ds(at, width)] = shifted(value, b - 1).astype(bf16)

    build(q + 1)

    @pl.when(y == 0)
    def _():
        cots[0] = jnp.zeros((chans, width), bf16)

    @pl.when(y == Y - 1)
    def _():
        cots[ZL + 1] = jnp.zeros((chans, width), bf16)

    for d in range(1, ZL):
        arrived(g2_piece(f, (q - d) % ZL), p_recv.at[d])
    gather_own(g2_block, b_send, b_recv)
    sends.append(send(g_block(f), g_block(f), a_send.at[0], a_recv.at[0], zh_dev))
    for d in range(ZL):
        arrived(g2_piece(partner, (q - d) % ZL), p_recv.at[ZL + d])
    gather_other(g2_block, b_send, b_recv)

    gather_third(g2_block, b_send, b_recv, 0)
    for d in range(1, ZL):
        arrived(cots.at[(q - d) % ZL + 1], c_recv.at[d])

    @pl.when(y < Y - 1)
    def _():
        halo_copy(0).start()

    @pl.when(y > 0)
    def _():
        halo_copy(1).start()

    for d in range(1, ZL):
        build((q - d) % ZL + 1)

    gather_third(g2_block, b_send, b_recv, 1)

    gather_last(g2_block, b_send, b_recv)

    arrived(g_block(partner), a_recv.at[0])
    gather_other(g_block, a_send, a_recv)

    def grad_term(a, first, last):
        at = (2 - a + first) * width
        return lax.dot_general(
            S[:, at : at + (last - first) * width], G2[:, first * width : last * width],
            (((1,), (1,)), ((), ())), preferred_element_type=f32,
        )

    dF[stack : 2 * stack, :] = grad_term(1, 0, ZL)
    dF[:stack, :] = grad_term(0, 0, ZL - 1)
    dF[2 * stack :, :] = grad_term(2, 1, ZL)

    @pl.when(y > 0)
    def _():
        arrived(cots.at[0], h_recv.at[0])

    @pl.when(y < Y - 1)
    def _():
        arrived(cots.at[ZL + 1], h_recv.at[1])

    build(0)
    build(ZL + 1)

    dF[:stack, :] += grad_term(0, ZL - 1, ZL)
    dF[2 * stack :, :] += grad_term(2, 0, 1)
    rows = TAPS * stack // Y
    scale = scale_for(dF[...])
    for k in range(Y):
        code, tail = pack(dF[rows * k : rows * (k + 1), :], scale)
        codes[k, : 2 * rows, :] = code
        codes[k, 2 * rows :, :] = tail
    for d in (4, 3, 5, 2, 6, 1, 7):
        sends.append(send(codes.at[(y + d) % Y], got.at[d], rs_send.at[d], rs_recv.at[d], y_peer(d)))

    load_f.wait()
    groups = X * ZH * CORES
    cols = width // groups
    half = width // 2
    for p in range(2):
        total = None
        for a in range(TAPS):
            at = pl.multiple_of((q + 2 - a) * width + p * half, half)
            term = lax.dot_general(
                S[:, pl.ds(at, half)], F2[a * stack : (a + 1) * stack, :],
                (((0,), (0,)), ((), ())), preferred_element_type=f32,
            )
            total = term if total is None else total + term
        for k in range(groups // 2):
            g = p * (groups // 2) + k
            IGB[g % CORES, g // (ZH * CORES), (g // CORES) % ZH] = total[cols * k : cols * (k + 1)]
    sends.append(send(IGB.at[1 - core], IGR, ig_send.at[0], ig_recv.at[0], core_dev))


    gather_third(g_block, a_send, a_recv, 0)
    gather_third(g_block, a_send, a_recv, 1)

    arrived(IGR, ig_recv.at[0])
    deep = ZH * cols
    for d in range(1, X):
        to = (x + d) % X
        code, tail = coded((IGB[core, to] + IGR[to]).reshape(deep, -1))
        IXC[d, :deep, :] = code
        IXC[d, deep:, :] = tail
        sends.append(send(IXC.at[d], IXR.at[d], ig_send.at[d], ig_recv.at[d], x_peer(d)))
    IGS[...] = IGB[core, x] + IGR[x]

    gather_last(g_block, a_send, a_recv)
    for a in (0, 2, 1):
        total = None
        taps = jnp.dot(F2[a * stack : (a + 1) * stack, :], G[...], preferred_element_type=f32)
        for b in range(TAPS):
            term = shifted(taps[b * chans : (b + 1) * chans], 1 - b)
            total = term if total is None else total + term
        if a == 1:
            O[...] = total
        else:
            code, tail = coded(total)
            OC[a // 2, :chans, :] = code
            OC[a // 2, chans:, :] = tail

    def out_copy(a):
        return pltpu.make_async_remote_copy(
            src_ref=OC.at[a // 2], dst_ref=OR.at[a // 2], send_sem=o_send.at[a // 2], recv_sem=o_recv.at[a // 2],
            device_id=dev(f, r + 1 - a), device_id_type=pl.DeviceIdType.MESH,
        )

    @pl.when(r < Y * ZL - 1)
    def _():
        out_copy(0).start()

    @pl.when(r > 0)
    def _():
        out_copy(2).start()

    piece = dF[pl.ds(pl.multiple_of(y * rows, rows), rows), :]
    for d in range(1, Y):
        arrived(got.at[d], rs_recv.at[d])
        piece = piece + unpack(got[d])
    piece = piece / jnp.sqrt(f32(Y * ZL * width))
    code, tail = pack(piece, scale_for(piece))
    FIN[y, q, : 2 * rows, :] = code
    FIN[y, q, 2 * rows :, :] = tail
    opposite = Y // 2

    def quarter(c):
        return (q + c) % ZL

    def ring(step, way, c):
        at = (y - (step - 1)) % Y if way == 0 else (y + (step - 1)) % Y
        ref = FIN.at[at, quarter(c)]
        to = y_peer(1 if way == 0 else -1)
        sends.append(send(ref, ref, fy_send.at[way, step, c], fy_recv.at[way, step, c], to))

    def ring_arrived(step, way, c):
        at = (y - step) % Y if way == 0 else (y + step) % Y
        arrived(FIN.at[at, quarter(c)], fy_recv.at[way, step, c])

    def pass_on(step, c):
        for way in range(2):
            ring_arrived(step, way, c)
            if step + 1 < opposite:
                ring(step + 1, way, c)

    def over_z(at, s_sem, r_sem):
        mine = FIN.at[at, q]
        for d in range(1, ZL):
            sends.append(send(mine, mine, s_sem.at[d], r_sem.at[d], zl_peer(d)))

    early = list(sends)
    sends.clear()
    over_z(y, fz_send, fz_recv)
    for way in range(2):
        ring(1, way, 0)
    sends.append(send(FIN.at[y, q], FIN.at[y, q], fo_send, fo_recv, y_peer(opposite)))

    pass_on(1, 0)
    for c in range(1, ZL):
        arrived(FIN.at[y, quarter(c)], fz_recv.at[ZL - c])
        for way in range(2):
            ring(1, way, c)
    across = (y + opposite) % Y
    arrived(FIN.at[across, q], fo_recv)
    over_z(across, fa_send, fa_recv)

    lane_group = lax.broadcasted_iota(jnp.int32, (rows, 128), 1) // 16

    def result(at):
        quarters = [unpack(FIN[at, k]) for k in range(ZL)]
        for t in range(8):
            half_at, j = t // 4, t % 4
            mine = (lane_group + (8 - j)) % ZL
            tile = quarters[0][:, 128 * half_at : 128 * (half_at + 1)]
            for k in range(1, ZL):
                tile = jnp.where(mine == k, quarters[k][:, 128 * half_at : 128 * (half_at + 1)], tile)
            if j:
                tile = pltpu.roll(tile, 128 - 16 * j, 1)
            fg_ref[pl.ds(pl.multiple_of(at * rows, 8), rows), 128 * t : 128 * (t + 1)] = tile

    result(y)
    for d in range(1, X):
        arrived(IXR.at[d], ig_recv.at[d])
        IGS[...] = IGS[...] + decoded(IXR[d]).reshape(IGS.shape)
    code, tail = coded(IGS[1 - zh])
    IZC[:cols, :] = code
    IZC[cols:, :] = tail
    sends.append(send(IZC, IZR, ig_send.at[X], ig_recv.at[X], zh_dev))
    for copy in early:
        copy.wait_send()

    for step in range(1, opposite):
        for c in range(1, ZL):
            pass_on(step, c)
        if step + 1 < opposite:
            pass_on(step + 1, 0)
        result((y - step) % Y)
        result((y + step) % Y)
    for c in range(1, ZL):
        arrived(FIN.at[across, quarter(c)], fa_recv.at[ZL - c])
    result(across)

    @pl.when(r > 0)
    def _():
        arrived(OR.at[0], o_recv.at[0])
        O[...] = O[...] + decoded(OR[0])

    @pl.when(r < Y * ZL - 1)
    def _():
        arrived(OR.at[1], o_recv.at[1])
        O[...] = O[...] + decoded(OR[1])

    out_ref[...] = O[...].astype(bf16)
    arrived(IZR, ig_recv.at[X])
    ig_ref[...] = (IGS[zh] + decoded(IZR[...])).astype(bf16)

    for copy in sends:
        copy.wait_send()

    @pl.when(y < Y - 1)
    def _():
        halo_copy(0).wait_send()

    @pl.when(y > 0)
    def _():
        halo_copy(1).wait_send()

    @pl.when(r < Y * ZL - 1)
    def _():
        out_copy(0).wait_send()

    @pl.when(r > 0)
    def _():
        out_copy(2).wait_send()


def on_device(images, filters, cotangent):
    _, chans, width = images.shape
    taps, total = filters.shape[1:]
    groups = X * ZH * CORES
    cols = width // groups
    stack = TAPS * chans
    piece = taps * chans // Y
    quarter = total // ZL
    dma = pltpu.SemaphoreType.DMA
    operands = images[0], jnp.transpose(filters, (1, 0, 2)).reshape(stack * TAPS, total), cotangent[0]
    vmem = pltpu.VMEM
    hbm_spec = pl.BlockSpec(memory_space=pltpu.HBM)
    vmem_spec = pl.BlockSpec(memory_space=pltpu.VMEM)
    code = (2 * piece + SCALE_ROWS, quarter // 2)
    output, input_grad, grad = pl.pallas_call(
        kernel,
        out_shape=(
            jax.ShapeDtypeStruct((chans, width), bf16),
            jax.ShapeDtypeStruct((cols, total), bf16),
            jax.ShapeDtypeStruct((taps * chans, total), f32),
        ),
        in_specs=[hbm_spec] * 3,
        out_specs=(vmem_spec, vmem_spec, vmem_spec),
        scratch_shapes=[
            vmem((taps * chans, total), bf16),
            vmem((total, width), bf16),
            vmem((quarter, ZL * width), bf16),
            vmem((ZL + 2, chans, width), bf16),
            vmem((stack, (ZL + 2) * width), bf16),
            vmem((taps * chans, quarter), f32),
            vmem((Y,) + code, bf16),
            vmem((Y,) + code, bf16),
            vmem((Y, ZL) + code, bf16),
            vmem((chans, width), f32),
            vmem((2, chans + SCALE_ROWS, width), bf16),
            vmem((2, chans + SCALE_ROWS, width), bf16),
            vmem((CORES, X, ZH, cols, total), f32),
            vmem((X, ZH, cols, total), f32),
            vmem((X, ZH * cols + SCALE_ROWS, total), bf16),
            vmem((X, ZH * cols + SCALE_ROWS, total), bf16),
            vmem((ZH, cols, total), f32),
            vmem((cols + SCALE_ROWS, total), bf16),
            vmem((cols + SCALE_ROWS, total), bf16),
            dma((3,)),
            dma((15,)), dma((15,)),
            dma((15,)), dma((15,)),
            dma((2 * ZL,)), dma((2 * ZL,)),
            dma((ZL,)), dma((ZL,)),
            dma((2,)), dma((2,)),
            dma((Y,)), dma((Y,)),
            dma((2,)), dma((2,)),
            dma((X + 1,)), dma((X + 1,)),
            dma((ZL,)), dma((ZL,)),
            dma((2, Y // 2, ZL)), dma((2, Y // 2, ZL)),
            dma, dma,
            dma((ZL,)), dma((ZL,)),
        ],
        compiler_params=pltpu.CompilerParams(
            collective_id=0, has_side_effects=True, vmem_limit_bytes=48 * 1024 * 1024
        ),
    )(*(pltpu.with_memory_space_constraint(a, pltpu.HBM) for a in operands))
    grad = jnp.transpose(grad.reshape(taps, chans, total), (1, 0, 2))
    return output[None], input_grad[None], grad


def solution(mesh):
    return jax.shard_map(
        on_device,
        mesh=mesh,
        in_specs=(P("rows", "filt", None), P("filt", None, None), P("rows", "filt", None)),
        out_specs=(P("rows", "filt", None), P("rows", "filt", None), P("filt", None, None)),
        check_vma=False,
    )
```

```python
import functools

import jax
import jax.numpy as jnp
from jax import lax
from jax.experimental import pallas as pl
from jax.experimental.pallas import tpu as pltpu
from jax.sharding import PartitionSpec as P

X, ZH, CORES = 4, 2, 2
Y, ZL = 8, 4
TAPS = 3
SCALE_ROWS = 16
TOP = 200.0
f32 = jnp.float32
bf16 = jnp.bfloat16


def shifted(value, by):
    if by == 0:
        return value
    width = value.shape[1]
    column = lax.broadcasted_iota(jnp.int32, value.shape, 1)
    rolled = pltpu.roll(value, by % width, 1)
    return jnp.where(column == (0 if by == 1 else width - 1), 0.0, rolled)


def scale_for(block):
    largest = jnp.max(jnp.abs(block), axis=(0, 1), keepdims=True)
    return (TOP / jnp.maximum(largest, 1e-30)).astype(bf16).astype(f32)


def encode(value, scale):
    t = value * scale
    t2 = t * t
    t4 = t2 * t2
    t8 = t4 * t4
    t16 = t8 * t8
    return jnp.where(t < 0.0, -t16, t16).astype(bf16)


def decode(code, inverse):
    c = code.astype(f32)
    a = jnp.abs(c)
    root = lax.rsqrt(lax.rsqrt(lax.rsqrt(lax.rsqrt(jnp.maximum(a, 1e-37)))))
    root = jnp.where(a < 1e-37, 0.0, root) * inverse
    return jnp.where(c < 0.0, -root, root)


def coded(value):
    scale = scale_for(value)
    return encode(value, scale), jnp.broadcast_to(scale, (SCALE_ROWS, value.shape[1])).astype(bf16)


def decoded(code):
    rows = code.shape[0] - SCALE_ROWS
    return decode(code[:rows, :], 1.0 / code[rows : rows + 1, :].astype(f32))


def pack(value, scale):
    lanes = value.shape[1] // 2
    flat = jnp.concatenate([value[:, :lanes], value[:, lanes:]], axis=0)
    return encode(flat, scale), jnp.broadcast_to(scale, (SCALE_ROWS, lanes)).astype(bf16)


def unpack(code):
    rows = code.shape[0] - SCALE_ROWS
    inverse = 1.0 / code[rows : rows + 1, :].astype(f32)
    flat = decode(code[:rows, :], inverse)
    return jnp.concatenate([flat[: rows // 2], flat[rows // 2 :]], axis=1)


def kernel(
    img_ref, filt_ref, cot_ref, out_ref, ig_ref, fg_ref,
    F2, G, G2, cots, S, dF, codes, got, FIN, O, OC, OR, IGB, IGR, IXC, IXR, IGS, IZC, IZR,
    f_sem, a_send, a_recv, b_send, b_recv, p_send, p_recv, c_send, c_recv, h_send, h_recv,
    rs_send, rs_recv, o_send, o_recv, ig_send, ig_recv, fz_send, fz_recv, fy_send, fy_recv,
    fo_send, fo_recv, fa_send, fa_recv,
):
    f, r = lax.axis_index("filt"), lax.axis_index("rows")
    x, zh, core = f // (ZH * CORES), (f // CORES) % ZH, f % CORES
    y, q = r // ZL, r % ZL
    chans, width = img_ref.shape
    part = chans // ZL
    stack = TAPS * chans

    def dev(f_to, r_to):
        return {"filt": f_to, "rows": r_to}

    def x_peer(d):
        return dev(((x + d) % X) * (ZH * CORES) + zh * CORES + core, r)

    def zl_peer(d):
        return dev(f, y * ZL + (q + d) % ZL)

    def y_peer(d):
        return dev(f, ((y + d) % Y) * ZL + q)

    partner = f + CORES - 2 * CORES * zh
    sibling = f + 1 - 2 * core
    zh_dev, core_dev = dev(partner, r), dev(sibling, r)

    sends = []

    def zh_peer(d):
        return dev(partner, y * ZL + (q + d) % ZL)

    def send(src, dst, s_sem, r_sem, to):
        copy = pltpu.make_async_remote_copy(
            src_ref=src, dst_ref=dst, send_sem=s_sem, recv_sem=r_sem,
            device_id=to, device_id_type=pl.DeviceIdType.MESH,
        )
        copy.start()
        return copy

    def arrived(dst, r_sem):
        pltpu.make_async_remote_copy(
            src_ref=dst, dst_ref=dst, send_sem=r_sem, recv_sem=r_sem,
            device_id=core_dev, device_id_type=pl.DeviceIdType.MESH,
        ).wait_recv()

    def g_block(k):
        return G.at[pl.ds(pl.multiple_of(k * chans, chans), chans), :]

    load_img = pltpu.make_async_copy(img_ref, g_block(f), f_sem.at[0])
    load_cot = pltpu.make_async_copy(cot_ref, cots.at[q + 1], f_sem.at[1])
    load_f = pltpu.make_async_copy(filt_ref, F2, f_sem.at[2])
    for load in (load_img, load_cot, load_f):
        load.start()

    barrier = pltpu.get_barrier_semaphore()

    def greet(to):
        pl.semaphore_signal(barrier, inc=1, device_id=to, device_id_type=pl.DeviceIdType.MESH)

    fixed = [zh_peer(d) for d in range(ZL)] + [y_peer(d) for d in (4, 3, 5, 2, 6, 1, 7)]
    fixed += [zl_peer(d) for d in range(1, ZL)] + [x_peer(d) for d in range(1, X)] + [core_dev]
    for to in fixed:
        greet(to)

    below, above = (y > 0) & (q == 0), (y < Y - 1) & (q == ZL - 1)

    @pl.when(below)
    def _():
        greet(dev(f, r - 1))

    @pl.when(above)
    def _():
        greet(dev(f, r + 1))

    def g2_rows(k, to=q):
        at = 8 * (k // 8) + (to + 4 * (k % 2) + (k % 8) // 2) % 8
        return pl.ds(pl.multiple_of(at * part, part), part)

    def g2_block(k):
        return G2.at[g2_rows(k), :]

    def g2_piece(k, row, to=q):
        return G2.at[g2_rows(k, to), pl.ds(pl.multiple_of(row * width, width), width)]

    load_img.wait()
    load_cot.wait()
    g2_piece(f, q)[...] = G[pl.ds(pl.multiple_of(f * chans + q * part, part), part), :]
    others = jnp.where(below, 1, 0) + jnp.where(above, 1, 0)
    pl.semaphore_wait(barrier, len(fixed) + others)

    for d in list(range(1, ZL)) + list(range(ZL, 2 * ZL)):
        to = (q + d) % ZL
        sends.append(send(
            G.at[pl.ds(pl.multiple_of(f * chans + to * part, part), part), :], g2_piece(f, q, to),
            p_send.at[d], p_recv.at[d], zl_peer(d) if d < ZL else zh_peer(d),
        ))

    def gather_own(block, s_sem, r_sem):
        mine = block(f)
        for d in (2, 1, 3):
            sends.append(send(mine, mine, s_sem.at[d], r_sem.at[d], x_peer(d)))
        sends.append(send(mine, mine, s_sem.at[4], r_sem.at[4], core_dev))

    def gather_other(block, s_sem, r_sem):
        other = block(partner)
        for d in (2, 1, 3):
            sends.append(send(other, other, s_sem.at[4 + d], r_sem.at[4 + d], x_peer(d)))
        sends.append(send(other, other, s_sem.at[8], r_sem.at[8], core_dev))

    def gather_third(block, s_sem, r_sem, second):
        for d in range(1, X):
            k = ((x - d) % X) * (ZH * CORES) + core + CORES * (zh if second == 0 else 1 - zh)
            theirs = block(k)
            arrived(theirs, r_sem.at[d + 4 * second])
            at = 9 + 2 * (d - 1) + second
            sends.append(send(theirs, theirs, s_sem.at[at], r_sem.at[at], core_dev))

    def gather_last(block, s_sem, r_sem):
        base = 1 - core
        arrived(block(sibling), r_sem.at[4])
        arrived(block(partner + 1 - 2 * core), r_sem.at[8])
        for d in range(1, X):
            x_from = ((x - d) % X) * (ZH * CORES) + base
            for second in range(2):
                k = x_from + CORES * (zh if second == 0 else 1 - zh)
                arrived(block(k), r_sem.at[9 + 2 * (d - 1) + second])

    for d in range(1, ZL):
        mine = cots.at[q + 1]
        sends.append(send(mine, mine, c_send.at[d], c_recv.at[d], zl_peer(d)))

    gather_own(g_block, a_send, a_recv)
    sends.append(send(g_block(f), g_block(f), a_send.at[0], a_recv.at[0], zh_dev))

    def halo_copy(side):
        source, slot, step = (ZL, 0, 1) if side == 0 else (1, ZL + 1, -1)
        return pltpu.make_async_remote_copy(
            src_ref=cots.at[source], dst_ref=cots.at[slot], send_sem=h_send.at[side],
            recv_sem=h_recv.at[side], device_id=y_peer(step), device_id_type=pl.DeviceIdType.MESH,
        )

    def build(j):
        value = cots[j].astype(f32)
        for b in range(TAPS):
            at = j * width if isinstance(j, int) else pl.multiple_of(j * width, width)
            S[b * chans : (b + 1) * chans, pl.ds(at, width)] = shifted(value, b - 1).astype(bf16)

    build(q + 1)

    @pl.when(y == 0)
    def _():
        cots[0] = jnp.zeros((chans, width), bf16)

    @pl.when(y == Y - 1)
    def _():
        cots[ZL + 1] = jnp.zeros((chans, width), bf16)

    for d in range(1, ZL):
        arrived(g2_piece(f, (q - d) % ZL), p_recv.at[d])
    gather_own(g2_block, b_send, b_recv)
    for d in range(ZL):
        arrived(g2_piece(partner, (q - d) % ZL), p_recv.at[ZL + d])
    gather_other(g2_block, b_send, b_recv)

    gather_third(g2_block, b_send, b_recv, 0)
    for d in range(1, ZL):
        arrived(cots.at[(q - d) % ZL + 1], c_recv.at[d])

    @pl.when(y < Y - 1)
    def _():
        halo_copy(0).start()

    @pl.when(y > 0)
    def _():
        halo_copy(1).start()

    for d in range(1, ZL):
        build((q - d) % ZL + 1)

    gather_third(g2_block, b_send, b_recv, 1)

    gather_last(g2_block, b_send, b_recv)

    arrived(g_block(partner), a_recv.at[0])
    gather_other(g_block, a_send, a_recv)

    def grad_term(a, first, last):
        at = (2 - a + first) * width
        return lax.dot_general(
            S[:, at : at + (last - first) * width], G2[:, first * width : last * width],
            (((1,), (1,)), ((), ())), preferred_element_type=f32,
        )

    dF[stack : 2 * stack, :] = grad_term(1, 0, ZL)
    dF[:stack, :] = grad_term(0, 0, ZL - 1)
    dF[2 * stack :, :] = grad_term(2, 1, ZL)

    @pl.when(y > 0)
    def _():
        arrived(cots.at[0], h_recv.at[0])

    @pl.when(y < Y - 1)
    def _():
        arrived(cots.at[ZL + 1], h_recv.at[1])

    build(0)
    build(ZL + 1)

    dF[:stack, :] += grad_term(0, ZL - 1, ZL)
    dF[2 * stack :, :] += grad_term(2, 0, 1)
    rows = TAPS * stack // Y
    scale = scale_for(dF[...])
    for k in range(Y):
        code, tail = pack(dF[rows * k : rows * (k + 1), :], scale)
        codes[k, : 2 * rows, :] = code
        codes[k, 2 * rows :, :] = tail
    for d in (4, 3, 5, 2, 6, 1, 7):
        sends.append(send(codes.at[(y + d) % Y], got.at[d], rs_send.at[d], rs_recv.at[d], y_peer(d)))

    load_f.wait()
    groups = X * ZH * CORES
    cols = width // groups
    half = width // 2
    for p in range(2):
        total = None
        for a in range(TAPS):
            at = pl.multiple_of((q + 2 - a) * width + p * half, half)
            term = lax.dot_general(
                S[:, pl.ds(at, half)], F2[a * stack : (a + 1) * stack, :],
                (((0,), (0,)), ((), ())), preferred_element_type=f32,
            )
            total = term if total is None else total + term
        for k in range(groups // 2):
            g = p * (groups // 2) + k
            IGB[g % CORES, g // (ZH * CORES), (g // CORES) % ZH] = total[cols * k : cols * (k + 1)]
    sends.append(send(IGB.at[1 - core], IGR, ig_send.at[0], ig_recv.at[0], core_dev))


    gather_third(g_block, a_send, a_recv, 0)
    gather_third(g_block, a_send, a_recv, 1)

    arrived(IGR, ig_recv.at[0])
    deep = ZH * cols
    for d in range(1, X):
        to = (x + d) % X
        code, tail = coded((IGB[core, to] + IGR[to]).reshape(deep, -1))
        IXC[d, :deep, :] = code
        IXC[d, deep:, :] = tail
        sends.append(send(IXC.at[d], IXR.at[d], ig_send.at[d], ig_recv.at[d], x_peer(d)))
    IGS[...] = IGB[core, x] + IGR[x]

    gather_last(g_block, a_send, a_recv)
    for a in (0, 2, 1):
        total = None
        taps = jnp.dot(F2[a * stack : (a + 1) * stack, :], G[...], preferred_element_type=f32)
        for b in range(TAPS):
            term = shifted(taps[b * chans : (b + 1) * chans], 1 - b)
            total = term if total is None else total + term
        if a == 1:
            O[...] = total
        else:
            code, tail = coded(total)
            OC[a // 2, :chans, :] = code
            OC[a // 2, chans:, :] = tail

    def out_copy(a):
        return pltpu.make_async_remote_copy(
            src_ref=OC.at[a // 2], dst_ref=OR.at[a // 2], send_sem=o_send.at[a // 2], recv_sem=o_recv.at[a // 2],
            device_id=dev(f, r + 1 - a), device_id_type=pl.DeviceIdType.MESH,
        )

    @pl.when(r < Y * ZL - 1)
    def _():
        out_copy(0).start()

    @pl.when(r > 0)
    def _():
        out_copy(2).start()

    piece = dF[pl.ds(pl.multiple_of(y * rows, rows), rows), :]
    for d in range(1, Y):
        arrived(got.at[d], rs_recv.at[d])
        piece = piece + unpack(got[d])
    piece = piece / jnp.sqrt(f32(Y * ZL * width))
    code, tail = pack(piece, scale_for(piece))
    FIN[y, q, : 2 * rows, :] = code
    FIN[y, q, 2 * rows :, :] = tail
    opposite = Y // 2

    def quarter(c):
        return (q + c) % ZL

    def ring(step, way, c):
        at = (y - (step - 1)) % Y if way == 0 else (y + (step - 1)) % Y
        ref = FIN.at[at, quarter(c)]
        to = y_peer(1 if way == 0 else -1)
        sends.append(send(ref, ref, fy_send.at[way, step, c], fy_recv.at[way, step, c], to))

    def ring_arrived(step, way, c):
        at = (y - step) % Y if way == 0 else (y + step) % Y
        arrived(FIN.at[at, quarter(c)], fy_recv.at[way, step, c])

    def pass_on(step, c):
        for way in range(2):
            ring_arrived(step, way, c)
            if step + 1 < opposite:
                ring(step + 1, way, c)

    def over_z(at, s_sem, r_sem):
        mine = FIN.at[at, q]
        for d in range(1, ZL):
            sends.append(send(mine, mine, s_sem.at[d], r_sem.at[d], zl_peer(d)))

    early = list(sends)
    sends.clear()
    over_z(y, fz_send, fz_recv)
    for way in range(2):
        ring(1, way, 0)
    sends.append(send(FIN.at[y, q], FIN.at[y, q], fo_send, fo_recv, y_peer(opposite)))

    pass_on(1, 0)
    for c in range(1, ZL):
        arrived(FIN.at[y, quarter(c)], fz_recv.at[ZL - c])
        for way in range(2):
            ring(1, way, c)
    across = (y + opposite) % Y
    arrived(FIN.at[across, q], fo_recv)
    over_z(across, fa_send, fa_recv)

    lane_group = lax.broadcasted_iota(jnp.int32, (rows, 128), 1) // 16

    def result(at):
        quarters = [unpack(FIN[at, k]) for k in range(ZL)]
        for t in range(8):
            half_at, j = t // 4, t % 4
            mine = (lane_group + (8 - j)) % ZL
            tile = quarters[0][:, 128 * half_at : 128 * (half_at + 1)]
            for k in range(1, ZL):
                tile = jnp.where(mine == k, quarters[k][:, 128 * half_at : 128 * (half_at + 1)], tile)
            if j:
                tile = pltpu.roll(tile, 128 - 16 * j, 1)
            fg_ref[pl.ds(pl.multiple_of(at * rows, 8), rows), 128 * t : 128 * (t + 1)] = tile

    result(y)
    for d in range(1, X):
        arrived(IXR.at[d], ig_recv.at[d])
        IGS[...] = IGS[...] + decoded(IXR[d]).reshape(IGS.shape)
    code, tail = coded(IGS[1 - zh])
    IZC[:cols, :] = code
    IZC[cols:, :] = tail
    sends.append(send(IZC, IZR, ig_send.at[X], ig_recv.at[X], zh_dev))
    for copy in early:
        copy.wait_send()

    def ring_step(step):
        for c in range(1, ZL):
            pass_on(step, c)
        if step + 1 < opposite:
            pass_on(step + 1, 0)
        result((y - step) % Y)
        result((y + step) % Y)

    for step in range(1, opposite - 1):
        ring_step(step)

    for c in range(1, ZL):
        arrived(FIN.at[across, quarter(c)], fa_recv.at[ZL - c])
    result(across)

    @pl.when(r > 0)
    def _():
        arrived(OR.at[0], o_recv.at[0])
        O[...] = O[...] + decoded(OR[0])

    @pl.when(r < Y * ZL - 1)
    def _():
        arrived(OR.at[1], o_recv.at[1])
        O[...] = O[...] + decoded(OR[1])

    out_ref[...] = O[...].astype(bf16)
    arrived(IZR, ig_recv.at[X])
    ig_ref[...] = (IGS[zh] + decoded(IZR[...])).astype(bf16)

    ring_step(opposite - 1)

    for copy in sends:
        copy.wait_send()

    @pl.when(y < Y - 1)
    def _():
        halo_copy(0).wait_send()

    @pl.when(y > 0)
    def _():
        halo_copy(1).wait_send()

    @pl.when(r < Y * ZL - 1)
    def _():
        out_copy(0).wait_send()

    @pl.when(r > 0)
    def _():
        out_copy(2).wait_send()


def on_device(images, filters, cotangent):
    _, chans, width = images.shape
    taps, total = filters.shape[1:]
    groups = X * ZH * CORES
    cols = width // groups
    stack = TAPS * chans
    piece = taps * chans // Y
    quarter = total // ZL
    dma = pltpu.SemaphoreType.DMA
    operands = images[0], jnp.transpose(filters, (1, 0, 2)).reshape(stack * TAPS, total), cotangent[0]
    vmem = pltpu.VMEM
    hbm_spec = pl.BlockSpec(memory_space=pltpu.HBM)
    vmem_spec = pl.BlockSpec(memory_space=pltpu.VMEM)
    code = (2 * piece + SCALE_ROWS, quarter // 2)
    output, input_grad, grad = pl.pallas_call(
        kernel,
        out_shape=(
            jax.ShapeDtypeStruct((chans, width), bf16),
            jax.ShapeDtypeStruct((cols, total), bf16),
            jax.ShapeDtypeStruct((taps * chans, total), f32),
        ),
        in_specs=[hbm_spec] * 3,
        out_specs=(vmem_spec, vmem_spec, vmem_spec),
        scratch_shapes=[
            vmem((taps * chans, total), bf16),
            vmem((total, width), bf16),
            vmem((quarter, ZL * width), bf16),
            vmem((ZL + 2, chans, width), bf16),
            vmem((stack, (ZL + 2) * width), bf16),
            vmem((taps * chans, quarter), f32),
            vmem((Y,) + code, bf16),
            vmem((Y,) + code, bf16),
            vmem((Y, ZL) + code, bf16),
            vmem((chans, width), f32),
            vmem((2, chans + SCALE_ROWS, width), bf16),
            vmem((2, chans + SCALE_ROWS, width), bf16),
            vmem((CORES, X, ZH, cols, total), f32),
            vmem((X, ZH, cols, total), f32),
            vmem((X, ZH * cols + SCALE_ROWS, total), bf16),
            vmem((X, ZH * cols + SCALE_ROWS, total), bf16),
            vmem((ZH, cols, total), f32),
            vmem((cols + SCALE_ROWS, total), bf16),
            vmem((cols + SCALE_ROWS, total), bf16),
            dma((3,)),
            dma((15,)), dma((15,)),
            dma((15,)), dma((15,)),
            dma((2 * ZL,)), dma((2 * ZL,)),
            dma((ZL,)), dma((ZL,)),
            dma((2,)), dma((2,)),
            dma((Y,)), dma((Y,)),
            dma((2,)), dma((2,)),
            dma((X + 1,)), dma((X + 1,)),
            dma((ZL,)), dma((ZL,)),
            dma((2, Y // 2, ZL)), dma((2, Y // 2, ZL)),
            dma, dma,
            dma((ZL,)), dma((ZL,)),
        ],
        compiler_params=pltpu.CompilerParams(
            collective_id=0, has_side_effects=True, vmem_limit_bytes=48 * 1024 * 1024
        ),
    )(*(pltpu.with_memory_space_constraint(a, pltpu.HBM) for a in operands))
    grad = jnp.transpose(grad.reshape(taps, chans, total), (1, 0, 2))
    return output[None], input_grad[None], grad


def solution(mesh):
    return jax.shard_map(
        on_device,
        mesh=mesh,
        in_specs=(P("rows", "filt", None), P("filt", None, None), P("rows", "filt", None)),
        out_specs=(P("rows", "filt", None), P("rows", "filt", None), P("filt", None, None)),
        check_vma=False,
    )
```

```python
import functools

import jax
import jax.numpy as jnp
from jax import lax
from jax.experimental import pallas as pl
from jax.experimental.pallas import tpu as pltpu
from jax.sharding import PartitionSpec as P

X, ZH, CORES = 4, 2, 2
Y, ZL = 8, 4
TAPS = 3
SCALE_ROWS = 16
TOP = 200.0
f32 = jnp.float32
bf16 = jnp.bfloat16


def shifted(value, by):
    if by == 0:
        return value
    width = value.shape[1]
    column = lax.broadcasted_iota(jnp.int32, value.shape, 1)
    rolled = pltpu.roll(value, by % width, 1)
    return jnp.where(column == (0 if by == 1 else width - 1), 0.0, rolled)


def scale_for(block):
    largest = jnp.max(jnp.abs(block), axis=(0, 1), keepdims=True)
    return (TOP / jnp.maximum(largest, 1e-30)).astype(bf16).astype(f32)


def encode(value, scale):
    t = value * scale
    t2 = t * t
    t4 = t2 * t2
    t8 = t4 * t4
    t16 = t8 * t8
    return jnp.where(t < 0.0, -t16, t16).astype(bf16)


def decode(code, inverse):
    c = code.astype(f32)
    a = jnp.abs(c)
    root = lax.rsqrt(lax.rsqrt(lax.rsqrt(lax.rsqrt(jnp.maximum(a, 1e-37)))))
    root = jnp.where(a < 1e-37, 0.0, root) * inverse
    return jnp.where(c < 0.0, -root, root)


def coded(value):
    scale = scale_for(value)
    return encode(value, scale), jnp.broadcast_to(scale, (SCALE_ROWS, value.shape[1])).astype(bf16)


def decoded(code):
    rows = code.shape[0] - SCALE_ROWS
    return decode(code[:rows, :], 1.0 / code[rows : rows + 1, :].astype(f32))


def pack(value, scale):
    lanes = value.shape[1] // 2
    flat = jnp.concatenate([value[:, :lanes], value[:, lanes:]], axis=0)
    return encode(flat, scale), jnp.broadcast_to(scale, (SCALE_ROWS, lanes)).astype(bf16)


def unpack(code):
    rows = code.shape[0] - SCALE_ROWS
    inverse = 1.0 / code[rows : rows + 1, :].astype(f32)
    flat = decode(code[:rows, :], inverse)
    return jnp.concatenate([flat[: rows // 2], flat[rows // 2 :]], axis=1)


def kernel(
    img_ref, filt_ref, cot_ref, out_ref, ig_ref, fg_ref,
    F2, G, G2, cots, S, dF, codes, got, FIN, O, OC, OR, IGB, IGR, IXC, IXR, IGS, IZC, IZR,
    f_sem, a_send, a_recv, b_send, b_recv, p_send, p_recv, c_send, c_recv, h_send, h_recv,
    rs_send, rs_recv, o_send, o_recv, ig_send, ig_recv, fz_send, fz_recv, fy_send, fy_recv,
    fo_send, fo_recv, fa_send, fa_recv,
):
    f, r = lax.axis_index("filt"), lax.axis_index("rows")
    x, zh, core = f // (ZH * CORES), (f // CORES) % ZH, f % CORES
    y, q = r // ZL, r % ZL
    chans, width = img_ref.shape
    part = chans // ZL
    stack = TAPS * chans

    def dev(f_to, r_to):
        return {"filt": f_to, "rows": r_to}

    def x_peer(d):
        return dev(((x + d) % X) * (ZH * CORES) + zh * CORES + core, r)

    def zl_peer(d):
        return dev(f, y * ZL + (q + d) % ZL)

    def y_peer(d):
        return dev(f, ((y + d) % Y) * ZL + q)

    z_first = ZL - 1 - (q + 1) // 2
    z_second = jnp.where((q == 0) | (q == ZL - 1), 2, 1)
    z_order = z_first, z_second, 6 - z_first - z_second

    partner = f + CORES - 2 * CORES * zh
    sibling = f + 1 - 2 * core
    zh_dev, core_dev = dev(partner, r), dev(sibling, r)

    sends = []

    def zh_peer(d):
        return dev(partner, y * ZL + (q + d) % ZL)

    def send(src, dst, s_sem, r_sem, to):
        copy = pltpu.make_async_remote_copy(
            src_ref=src, dst_ref=dst, send_sem=s_sem, recv_sem=r_sem,
            device_id=to, device_id_type=pl.DeviceIdType.MESH,
        )
        copy.start()
        return copy

    def arrived(dst, r_sem):
        pltpu.make_async_remote_copy(
            src_ref=dst, dst_ref=dst, send_sem=r_sem, recv_sem=r_sem,
            device_id=core_dev, device_id_type=pl.DeviceIdType.MESH,
        ).wait_recv()

    def g_block(k):
        return G.at[pl.ds(pl.multiple_of(k * chans, chans), chans), :]

    load_img = pltpu.make_async_copy(img_ref, g_block(f), f_sem.at[0])
    load_cot = pltpu.make_async_copy(cot_ref, cots.at[q + 1], f_sem.at[1])
    load_f = pltpu.make_async_copy(filt_ref, F2, f_sem.at[2])
    for load in (load_img, load_cot, load_f):
        load.start()

    barrier = pltpu.get_barrier_semaphore()

    def greet(to):
        pl.semaphore_signal(barrier, inc=1, device_id=to, device_id_type=pl.DeviceIdType.MESH)

    fixed = [zh_peer(d) for d in range(ZL)] + [y_peer(d) for d in (4, 3, 5, 2, 6, 1, 7)]
    fixed += [zl_peer(d) for d in range(1, ZL)] + [x_peer(d) for d in range(1, X)] + [core_dev]
    for to in fixed:
        greet(to)

    below, above = (y > 0) & (q == 0), (y < Y - 1) & (q == ZL - 1)

    @pl.when(below)
    def _():
        greet(dev(f, r - 1))

    @pl.when(above)
    def _():
        greet(dev(f, r + 1))

    def g2_rows(k, to=q):
        at = 8 * (k // 8) + (to + 4 * (k % 2) + (k % 8) // 2) % 8
        return pl.ds(pl.multiple_of(at * part, part), part)

    def g2_block(k):
        return G2.at[g2_rows(k), :]

    def g2_piece(k, row, to=q):
        return G2.at[g2_rows(k, to), pl.ds(pl.multiple_of(row * width, width), width)]

    load_img.wait()
    load_cot.wait()
    g2_piece(f, q)[...] = G[pl.ds(pl.multiple_of(f * chans + q * part, part), part), :]
    others = jnp.where(below, 1, 0) + jnp.where(above, 1, 0)
    pl.semaphore_wait(barrier, len(fixed) + others)

    for d in list(range(1, ZL)) + list(range(ZL, 2 * ZL)):
        to = (q + d) % ZL
        sends.append(send(
            G.at[pl.ds(pl.multiple_of(f * chans + to * part, part), part), :], g2_piece(f, q, to),
            p_send.at[d], p_recv.at[d], zl_peer(d) if d < ZL else zh_peer(d),
        ))

    def gather_own(block, s_sem, r_sem):
        mine = block(f)
        for d in (2, 1, 3):
            sends.append(send(mine, mine, s_sem.at[d], r_sem.at[d], x_peer(d)))
        sends.append(send(mine, mine, s_sem.at[4], r_sem.at[4], core_dev))

    def gather_other(block, s_sem, r_sem):
        other = block(partner)
        for d in (2, 1, 3):
            sends.append(send(other, other, s_sem.at[4 + d], r_sem.at[4 + d], x_peer(d)))
        sends.append(send(other, other, s_sem.at[8], r_sem.at[8], core_dev))

    def gather_third(block, s_sem, r_sem, second):
        for d in range(1, X):
            k = ((x - d) % X) * (ZH * CORES) + core + CORES * (zh if second == 0 else 1 - zh)
            theirs = block(k)
            arrived(theirs, r_sem.at[d + 4 * second])
            at = 9 + 2 * (d - 1) + second
            sends.append(send(theirs, theirs, s_sem.at[at], r_sem.at[at], core_dev))

    def gather_last(block, s_sem, r_sem):
        base = 1 - core
        arrived(block(sibling), r_sem.at[4])
        arrived(block(partner + 1 - 2 * core), r_sem.at[8])
        for d in range(1, X):
            x_from = ((x - d) % X) * (ZH * CORES) + base
            for second in range(2):
                k = x_from + CORES * (zh if second == 0 else 1 - zh)
                arrived(block(k), r_sem.at[9 + 2 * (d - 1) + second])

    for d in z_order:
        mine = cots.at[q + 1]
        sends.append(send(mine, mine, c_send.at[d], c_recv.at[d], zl_peer(d)))

    gather_own(g_block, a_send, a_recv)
    sends.append(send(g_block(f), g_block(f), a_send.at[0], a_recv.at[0], zh_dev))

    def halo_copy(side):
        source, slot, step = (ZL, 0, 1) if side == 0 else (1, ZL + 1, -1)
        return pltpu.make_async_remote_copy(
            src_ref=cots.at[source], dst_ref=cots.at[slot], send_sem=h_send.at[side],
            recv_sem=h_recv.at[side], device_id=y_peer(step), device_id_type=pl.DeviceIdType.MESH,
        )

    def build(j):
        value = cots[j].astype(f32)
        for b in range(TAPS):
            at = j * width if isinstance(j, int) else pl.multiple_of(j * width, width)
            S[b * chans : (b + 1) * chans, pl.ds(at, width)] = shifted(value, b - 1).astype(bf16)

    build(q + 1)

    @pl.when(y == 0)
    def _():
        cots[0] = jnp.zeros((chans, width), bf16)

    @pl.when(y == Y - 1)
    def _():
        cots[ZL + 1] = jnp.zeros((chans, width), bf16)

    for d in range(1, ZL):
        arrived(g2_piece(f, (q - d) % ZL), p_recv.at[d])
    gather_own(g2_block, b_send, b_recv)
    for d in range(ZL):
        arrived(g2_piece(partner, (q - d) % ZL), p_recv.at[ZL + d])
    gather_other(g2_block, b_send, b_recv)

    gather_third(g2_block, b_send, b_recv, 0)
    for d in range(1, ZL):
        arrived(cots.at[(q - d) % ZL + 1], c_recv.at[d])

    @pl.when(y < Y - 1)
    def _():
        halo_copy(0).start()

    @pl.when(y > 0)
    def _():
        halo_copy(1).start()

    for d in range(1, ZL):
        build((q - d) % ZL + 1)

    gather_third(g2_block, b_send, b_recv, 1)

    gather_last(g2_block, b_send, b_recv)

    arrived(g_block(partner), a_recv.at[0])
    gather_other(g_block, a_send, a_recv)

    def grad_term(a, first, last):
        at = (2 - a + first) * width
        return lax.dot_general(
            S[:, at : at + (last - first) * width], G2[:, first * width : last * width],
            (((1,), (1,)), ((), ())), preferred_element_type=f32,
        )

    dF[stack : 2 * stack, :] = grad_term(1, 0, ZL)
    dF[:stack, :] = grad_term(0, 0, ZL - 1)
    dF[2 * stack :, :] = grad_term(2, 1, ZL)

    @pl.when(y > 0)
    def _():
        arrived(cots.at[0], h_recv.at[0])

    @pl.when(y < Y - 1)
    def _():
        arrived(cots.at[ZL + 1], h_recv.at[1])

    build(0)
    build(ZL + 1)

    dF[:stack, :] += grad_term(0, ZL - 1, ZL)
    dF[2 * stack :, :] += grad_term(2, 0, 1)
    rows = TAPS * stack // Y
    scale = scale_for(dF[...])
    for d in (4, 3, 5, 2, 6, 1, 7):
        at = pl.multiple_of(((y + d) % Y) * rows, rows)
        code, tail = pack(dF[pl.ds(at, rows), :], scale)
        codes[d, : 2 * rows, :] = code
        codes[d, 2 * rows :, :] = tail
        sends.append(send(codes.at[d], got.at[d], rs_send.at[d], rs_recv.at[d], y_peer(d)))

    load_f.wait()
    groups = X * ZH * CORES
    cols = width // groups
    half = width // 2
    for p in range(2):
        total = None
        for a in range(TAPS):
            at = pl.multiple_of((q + 2 - a) * width + p * half, half)
            term = lax.dot_general(
                S[:, pl.ds(at, half)], F2[a * stack : (a + 1) * stack, :],
                (((0,), (0,)), ((), ())), preferred_element_type=f32,
            )
            total = term if total is None else total + term
        for k in range(groups // 2):
            g = p * (groups // 2) + k
            IGB[g % CORES, g // (ZH * CORES), (g // CORES) % ZH] = total[cols * k : cols * (k + 1)]
    sends.append(send(IGB.at[1 - core], IGR, ig_send.at[0], ig_recv.at[0], core_dev))


    gather_third(g_block, a_send, a_recv, 0)
    gather_third(g_block, a_send, a_recv, 1)

    arrived(IGR, ig_recv.at[0])
    deep = ZH * cols
    for d in range(1, X):
        to = (x + d) % X
        code, tail = coded((IGB[core, to] + IGR[to]).reshape(deep, -1))
        IXC[d, :deep, :] = code
        IXC[d, deep:, :] = tail
        sends.append(send(IXC.at[d], IXR.at[d], ig_send.at[d], ig_recv.at[d], x_peer(d)))
    IGS[...] = IGB[core, x] + IGR[x]

    gather_last(g_block, a_send, a_recv)
    for a in (0, 2, 1):
        total = None
        taps = jnp.dot(F2[a * stack : (a + 1) * stack, :], G[...], preferred_element_type=f32)
        for b in range(TAPS):
            term = shifted(taps[b * chans : (b + 1) * chans], 1 - b)
            total = term if total is None else total + term
        if a == 1:
            O[...] = total
        else:
            code, tail = coded(total)
            OC[a // 2, :chans, :] = code
            OC[a // 2, chans:, :] = tail

    def out_copy(a):
        return pltpu.make_async_remote_copy(
            src_ref=OC.at[a // 2], dst_ref=OR.at[a // 2], send_sem=o_send.at[a // 2], recv_sem=o_recv.at[a // 2],
            device_id=dev(f, r + 1 - a), device_id_type=pl.DeviceIdType.MESH,
        )

    @pl.when(r < Y * ZL - 1)
    def _():
        out_copy(0).start()

    @pl.when(r > 0)
    def _():
        out_copy(2).start()

    piece = dF[pl.ds(pl.multiple_of(y * rows, rows), rows), :]
    for d in range(1, Y):
        arrived(got.at[d], rs_recv.at[d])
        piece = piece + unpack(got[d])
    piece = piece / jnp.sqrt(f32(Y * ZL * width))
    code, tail = pack(piece, scale_for(piece))
    FIN[y, q, : 2 * rows, :] = code
    FIN[y, q, 2 * rows :, :] = tail
    opposite = Y // 2

    def quarter(c):
        return (q + c) % ZL

    def ring(step, way, c):
        at = (y - (step - 1)) % Y if way == 0 else (y + (step - 1)) % Y
        ref = FIN.at[at, quarter(c)]
        to = y_peer(1 if way == 0 else -1)
        sends.append(send(ref, ref, fy_send.at[way, step, c], fy_recv.at[way, step, c], to))

    def ring_arrived(step, way, c):
        at = (y - step) % Y if way == 0 else (y + step) % Y
        arrived(FIN.at[at, quarter(c)], fy_recv.at[way, step, c])

    def pass_on(step, c):
        for way in range(2):
            ring_arrived(step, way, c)
            if step + 1 < opposite:
                ring(step + 1, way, c)

    def over_z(at, s_sem, r_sem):
        mine = FIN.at[at, q]
        for d in z_order:
            sends.append(send(mine, mine, s_sem.at[d], r_sem.at[d], zl_peer(d)))

    early = list(sends)
    sends.clear()
    over_z(y, fz_send, fz_recv)
    for way in range(2):
        ring(1, way, 0)
    sends.append(send(FIN.at[y, q], FIN.at[y, q], fo_send, fo_recv, y_peer(opposite)))

    pass_on(1, 0)
    for c in range(1, ZL):
        arrived(FIN.at[y, quarter(c)], fz_recv.at[ZL - c])
        for way in range(2):
            ring(1, way, c)
    across = (y + opposite) % Y
    arrived(FIN.at[across, q], fo_recv)
    over_z(across, fa_send, fa_recv)

    lane_group = lax.broadcasted_iota(jnp.int32, (rows, 128), 1) // 16

    def result(at):
        quarters = [unpack(FIN[at, k]) for k in range(ZL)]
        for t in range(8):
            half_at, j = t // 4, t % 4
            mine = (lane_group + (8 - j)) % ZL
            tile = quarters[0][:, 128 * half_at : 128 * (half_at + 1)]
            for k in range(1, ZL):
                tile = jnp.where(mine == k, quarters[k][:, 128 * half_at : 128 * (half_at + 1)], tile)
            if j:
                tile = pltpu.roll(tile, 128 - 16 * j, 1)
            fg_ref[pl.ds(pl.multiple_of(at * rows, 8), rows), 128 * t : 128 * (t + 1)] = tile

    result(y)
    for d in range(1, X):
        arrived(IXR.at[d], ig_recv.at[d])
        IGS[...] = IGS[...] + decoded(IXR[d]).reshape(IGS.shape)
    code, tail = coded(IGS[1 - zh])
    IZC[:cols, :] = code
    IZC[cols:, :] = tail
    sends.append(send(IZC, IZR, ig_send.at[X], ig_recv.at[X], zh_dev))
    for copy in early:
        copy.wait_send()

    def ring_step(step):
        for c in range(1, ZL):
            pass_on(step, c)
        if step + 1 < opposite:
            pass_on(step + 1, 0)
        result((y - step) % Y)
        result((y + step) % Y)

    for step in range(1, opposite - 1):
        ring_step(step)

    for c in range(1, ZL):
        arrived(FIN.at[across, quarter(c)], fa_recv.at[ZL - c])
    result(across)

    @pl.when(r > 0)
    def _():
        arrived(OR.at[0], o_recv.at[0])
        O[...] = O[...] + decoded(OR[0])

    @pl.when(r < Y * ZL - 1)
    def _():
        arrived(OR.at[1], o_recv.at[1])
        O[...] = O[...] + decoded(OR[1])

    out_ref[...] = O[...].astype(bf16)
    arrived(IZR, ig_recv.at[X])
    ig_ref[...] = (IGS[zh] + decoded(IZR[...])).astype(bf16)

    ring_step(opposite - 1)

    for copy in sends:
        copy.wait_send()

    @pl.when(y < Y - 1)
    def _():
        halo_copy(0).wait_send()

    @pl.when(y > 0)
    def _():
        halo_copy(1).wait_send()

    @pl.when(r < Y * ZL - 1)
    def _():
        out_copy(0).wait_send()

    @pl.when(r > 0)
    def _():
        out_copy(2).wait_send()


def on_device(images, filters, cotangent):
    _, chans, width = images.shape
    taps, total = filters.shape[1:]
    groups = X * ZH * CORES
    cols = width // groups
    stack = TAPS * chans
    piece = taps * chans // Y
    quarter = total // ZL
    dma = pltpu.SemaphoreType.DMA
    operands = images[0], jnp.transpose(filters, (1, 0, 2)).reshape(stack * TAPS, total), cotangent[0]
    vmem = pltpu.VMEM
    hbm_spec = pl.BlockSpec(memory_space=pltpu.HBM)
    vmem_spec = pl.BlockSpec(memory_space=pltpu.VMEM)
    code = (2 * piece + SCALE_ROWS, quarter // 2)
    output, input_grad, grad = pl.pallas_call(
        kernel,
        out_shape=(
            jax.ShapeDtypeStruct((chans, width), bf16),
            jax.ShapeDtypeStruct((cols, total), bf16),
            jax.ShapeDtypeStruct((taps * chans, total), f32),
        ),
        in_specs=[hbm_spec] * 3,
        out_specs=(vmem_spec, vmem_spec, vmem_spec),
        scratch_shapes=[
            vmem((taps * chans, total), bf16),
            vmem((total, width), bf16),
            vmem((quarter, ZL * width), bf16),
            vmem((ZL + 2, chans, width), bf16),
            vmem((stack, (ZL + 2) * width), bf16),
            vmem((taps * chans, quarter), f32),
            vmem((Y,) + code, bf16),
            vmem((Y,) + code, bf16),
            vmem((Y, ZL) + code, bf16),
            vmem((chans, width), f32),
            vmem((2, chans + SCALE_ROWS, width), bf16),
            vmem((2, chans + SCALE_ROWS, width), bf16),
            vmem((CORES, X, ZH, cols, total), f32),
            vmem((X, ZH, cols, total), f32),
            vmem((X, ZH * cols + SCALE_ROWS, total), bf16),
            vmem((X, ZH * cols + SCALE_ROWS, total), bf16),
            vmem((ZH, cols, total), f32),
            vmem((cols + SCALE_ROWS, total), bf16),
            vmem((cols + SCALE_ROWS, total), bf16),
            dma((3,)),
            dma((15,)), dma((15,)),
            dma((15,)), dma((15,)),
            dma((2 * ZL,)), dma((2 * ZL,)),
            dma((ZL,)), dma((ZL,)),
            dma((2,)), dma((2,)),
            dma((Y,)), dma((Y,)),
            dma((2,)), dma((2,)),
            dma((X + 1,)), dma((X + 1,)),
            dma((ZL,)), dma((ZL,)),
            dma((2, Y // 2, ZL)), dma((2, Y // 2, ZL)),
            dma, dma,
            dma((ZL,)), dma((ZL,)),
        ],
        compiler_params=pltpu.CompilerParams(
            collective_id=0, has_side_effects=True, vmem_limit_bytes=48 * 1024 * 1024
        ),
    )(*(pltpu.with_memory_space_constraint(a, pltpu.HBM) for a in operands))
    grad = jnp.transpose(grad.reshape(taps, chans, total), (1, 0, 2))
    return output[None], input_grad[None], grad


def solution(mesh):
    return jax.shard_map(
        on_device,
        mesh=mesh,
        in_specs=(P("rows", "filt", None), P("filt", None, None), P("rows", "filt", None)),
        out_specs=(P("rows", "filt", None), P("rows", "filt", None), P("filt", None, None)),
        check_vma=False,
    )
```
